32 devices in a mesh: groups: 2 (over y), ra: 4 (over z), dec: 2 (over x), band: 2 (over core).
Axes of the slice: x: 2, y: 2, z: 4, core: 2. Of those that a mesh axis runs over, the one named last changes fastest.
Arguments:
- sky_maps: bfloat16 [512, 312, 256], P(('groups', 'band'), 'ra', 'dec'), parts along dimension 0, may hold values from -12 to 12
- radii: int32 [512], P(('groups', 'band')), parts along dimension 0, may hold values from 1 to 17, as said below
- valid: int32 [624, 256], P(('groups', 'ra'), 'dec'), parts along dimension 0, may hold values from 0 to 1, as said below
Outputs:
- smoothed: bfloat16 [512, 312, 256], P(('groups', 'band'), 'ra', 'dec'), parts along dimension 0
- channel_mean: float32 [512], P(('groups', 'band')), parts along dimension 0
- covariance: float32 [512, 256], P('groups', 'band'), parts along dimension 0
The draws below stay inside these ranges and needn't reach their ends.
There are 2 independent parts, one for each index of `groups`. The reference program is written for one: setup_inputs(seed, part) draws one part's arguments, and reference() takes and returns one part's arrays. A program takes and returns all parts, laid end to end along the dimension named above; each array names one. Nothing has to cross between parts.
Inputs may be any that keep to these rules, and one draw needn't show every extreme that they name: `radii`: some channel has half-width exactly 17. 1 marks a pixel that enters the statistics; the pixel with declination index 0 is valid in every row.
All inputs are finite; a program needn't handle non-finite values.
Results may differ from the reference program's by a relative error of at most 0.012.
The reference program's roundings to bfloat16 on the way count: a program that leaves them out, or rounds other values in their place, can miss the bound.
Values may be sent and summed in bfloat16 or wider, within the bound.
A program may use at most 64 MiB of HBM per device.

```python
import jax
import jax.numpy as jnp
from jax import lax

CHANNELS = 256
RMAX = 17
NRA = 312
NDEC = 256


def draw_sky_maps(key, part):
    noise_key = jax.random.fold_in(key, 11)
    full_shape = (CHANNELS, NRA, NDEC)
    values = jax.random.normal(noise_key, full_shape, jnp.float32)
    return jnp.clip(values, -12.0, 12.0).astype(jnp.bfloat16)


def draw_radii(key, part):
    pick_key = jax.random.fold_in(key, 21)
    place_key = jax.random.fold_in(key, 22)
    values = jax.random.randint(pick_key, (CHANNELS,), 1, RMAX + 1)
    place = jax.random.randint(place_key, (), 0, CHANNELS)
    return jnp.where(jnp.arange(CHANNELS) == place, RMAX, values).astype(jnp.int32)


def draw_valid(key, part):
    full_shape = (NRA, NDEC)
    along = lax.broadcasted_iota(jnp.int32, full_shape, 0)
    down = lax.broadcasted_iota(jnp.int32, full_shape, 1)
    chance = 200 + 400 * along // NRA + 300 * down // NDEC
    coins = jax.random.randint(jax.random.fold_in(key, 31), full_shape, 0, 1000)
    picked = (coins < chance) | (down == 0)
    return jnp.where(picked, 1, 0).astype(jnp.int32)


def setup_inputs(seed: int = 0, part: int = 0) -> dict:
    seeds = jax.random.split(jax.random.key(seed), 4)
    part_keys = jax.random.split(jax.random.fold_in(seeds[3], part), 4)
    return {
        "sky_maps": draw_sky_maps(jax.random.fold_in(jax.random.fold_in(seeds[3], part), 71), part),
        "radii": draw_radii(jax.random.fold_in(jax.random.fold_in(seeds[3], part), 71), part),
        "valid": draw_valid(jax.random.fold_in(jax.random.fold_in(seeds[3], part), 71), part),
    }


def beam_taps(radii, offsets):
    radius = radii.astype(jnp.float32)
    lead_shape = (radii.shape[0],) + (1,) * offsets.ndim
    radius = radius.reshape(lead_shape)
    spread = 0.5 * radius
    inside = jnp.abs(offsets)[None] <= radius
    return jnp.where(inside, jnp.exp(-(offsets * offsets)[None] / (2.0 * spread * spread)), 0.0)


def reference(sky_maps, radii, valid):
    raw_taps = beam_taps(radii, jnp.arange(-RMAX, RMAX + 1).astype(jnp.float32))
    kernel_taps = (raw_taps / jnp.sum(raw_taps, axis=1)[:, None]).astype(jnp.bfloat16)

    def smooth_one(item):
        plane, weights = item
        values = plane.astype(jnp.float32)
        kernel = weights.astype(jnp.float32)
        padded = jnp.pad(values, ((0, 0), (RMAX, RMAX)))
        across = jnp.zeros(values.shape, jnp.float32)
        for index in range(2 * RMAX + 1):
            across = across + kernel[index] * padded[:, index:index + NDEC]
        across = lax.optimization_barrier(across.astype(jnp.bfloat16)).astype(jnp.float32)
        result = jnp.zeros(values.shape, jnp.float32)
        for index in range(2 * RMAX + 1):
            result = result + kernel[index] * jnp.roll(across, -(index - RMAX), axis=0)
        return result.astype(jnp.bfloat16)

    smoothed = lax.map(smooth_one, (sky_maps, kernel_taps))
    flat = smoothed.reshape(smoothed.shape[0], -1)
    weights = valid.reshape(-1).astype(jnp.float32)
    masked = flat * weights.astype(jnp.bfloat16)[None]
    sums = jnp.sum(masked.astype(jnp.float32), axis=1)
    count = jnp.sum(weights)
    channel_mean = sums / count
    gram = lax.dot_general(masked, masked, (((1,), (1,)), ((), ())), preferred_element_type=jnp.float32)
    covariance = (gram - count * channel_mean[:, None] * channel_mean[None, :]) / (count - 1.0)
    return smoothed, channel_mean, covariance
```

```python
import functools

import jax
import jax.numpy as jnp
from jax import lax
from jax.experimental import pallas as pl
from jax.experimental.pallas import tpu as pltpu
from jax.sharding import PartitionSpec as P

RMAX = 17
WIDE = RMAX + 1
CB = 16
EARLY = 2
MESH = pl.DeviceIdType.MESH


def up(value, step):
    return -(-value // step) * step


def iota(shape, dim):
    return lax.broadcasted_iota(jnp.int32, shape, dim)


def early_blocks(blocks):
    return min(EARLY, blocks - 1)


def inner_rows(rows):
    first = RMAX // 16 * 16
    last = up(rows - RMAX, 16)
    return first, last - first, up(RMAX, 8)


def kernel(
    dims, radii_hbm, sky_hbm, valid_hbm, out_ref, mean_ref, cov_ref,
    sky_ref, valid_ref, radii_ref, loads,
    tab_dec, tab_in, tab_ed, xs, hs, os, ps, vb, mine_in, mine_ed, other_in, other_ed,
    pack_up, pack_dn, halo_lo, halo_hi, far_up, far_dn, far_lo, far_hi, edge_lo, edge_hi, z_before, z_after,
    acc, shares, total, aux, aux_all,
    s_dec, r_dec, s_ra, r_ra, s_band, r_band, s_rs, r_rs, s_ag, r_ag, s_aux, r_aux,
):
    n_ra, n_dec, rows, chans, cols = dims
    blocks = chans // CB
    rows8 = up(rows, 16)
    groups = cols // WIDE
    per = -(-rows // groups)
    far_per = -(-2 * RMAX // groups)
    late = blocks - early_blocks(blocks)
    peers = n_ra * n_dec
    reducers = min(peers, chans // 8)
    share = chans // reducers
    ext = 128
    in_at, in_rows, edge_rows = inner_rows(rows)
    ra, dec, band = lax.axis_index("ra"), lax.axis_index("dec"), lax.axis_index("band")
    rank = ra * n_dec + dec
    nxt, prv = lax.rem(ra + 1, n_ra), lax.rem(ra + n_ra - 1, n_ra)
    twin = {"band": 1 - band}

    def peer_id(p):
        return {"ra": p // n_dec, "dec": lax.rem(p, n_dec)}

    def each_peer(body):
        def step(d, carry):
            body(lax.rem(rank + d, peers))
            return carry
        lax.fori_loop(1, peers, step, 0)

    def table(r, carry):
        radius = r.astype(jnp.float32)
        spread = 0.5 * radius
        k = lax.rem(iota((8, cols), 0) - iota((8, cols), 1) + cols + cols // 2, cols) - cols // 2
        k = k.astype(jnp.float32)
        raw = jnp.where(jnp.abs(k) <= radius, jnp.exp(-(k * k) / (2.0 * spread * spread)), 0.0)
        first = raw / jnp.sum(raw, axis=1, keepdims=True)
        full = jnp.concatenate([pltpu.roll(first, 8 * t, 1) for t in range(cols // 8)], axis=0)
        near = jnp.abs(iota((cols, cols), 0) - iota((cols, cols), 1)) <= cols // 2
        tab_in[r] = full[in_at:in_at + in_rows].astype(jnp.bfloat16)
        ends = jnp.concatenate([full[0:edge_rows], full[rows8 - edge_rows:rows8]], axis=0)
        tab_ed[r] = ends.astype(jnp.bfloat16)
        tab_dec[r, 0:cols, :] = jnp.where(near, full, 0.0).astype(jnp.bfloat16)
        tab_dec[r, cols:2 * cols, :] = jnp.where(near, 0.0, full).astype(jnp.bfloat16)
        return carry

    def load_sky(b):
        at = pl.multiple_of(b * CB, CB)
        return pltpu.make_async_copy(
            sky_hbm.at[:, pl.ds(at, CB), :], sky_ref.at[:, pl.ds(at, CB), :], loads.at[b]
        )

    load_valid = pltpu.make_async_copy(valid_hbm, valid_ref, loads.at[blocks])
    load_radii = pltpu.make_async_copy(radii_hbm, radii_ref, loads.at[blocks + 1])
    barrier = pltpu.get_barrier_semaphore()
    each_peer(lambda p: pl.semaphore_signal(barrier, inc=1, device_id=peer_id(p), device_id_type=MESH))
    pl.semaphore_signal(barrier, inc=1, device_id=twin, device_id_type=MESH)

    def for_blocks(body, first=0, last=blocks):
        def step(b, carry):
            body(b)
            return carry
        lax.fori_loop(first, last, step, 0)

    for_blocks(lambda b: load_sky(b).start())
    load_valid.start()
    load_radii.start()
    pl.semaphore_wait(barrier, peers)

    def remote(src, dst, send, recv, target):
        return pltpu.make_async_remote_copy(
            src_ref=src, dst_ref=dst, send_sem=send, recv_sem=recv, device_id=target, device_id_type=MESH
        )

    def dec_up(b):
        return remote(pack_up.at[b], halo_lo.at[b], s_dec.at[0, b], r_dec.at[0, b], {"dec": dec + 1})

    def dec_dn(b):
        return remote(pack_dn.at[b], halo_hi.at[b], s_dec.at[1, b], r_dec.at[1, b], {"dec": dec - 1})

    def far_dec_up(j):
        return remote(
            far_up.at[j], far_lo.at[j], s_dec.at[0, blocks + j], r_dec.at[0, blocks + j], {"dec": dec + 1}
        )

    def far_dec_dn(j):
        return remote(
            far_dn.at[j], far_hi.at[j], s_dec.at[1, blocks + j], r_dec.at[1, blocks + j], {"dec": dec - 1}
        )

    def sky_up(b):
        rim = sky_hbm.at[pl.ds(rows - RMAX, RMAX), pl.ds(pl.multiple_of(b * CB, CB), CB), :]
        return remote(rim, z_before.at[b], s_ra.at[0, b], r_ra.at[0, b], {"ra": nxt})

    def sky_dn(b):
        rim = sky_hbm.at[pl.ds(0, RMAX), pl.ds(pl.multiple_of(b * CB, CB), CB), :]
        return remote(rim, z_after.at[b], s_ra.at[1, b], r_ra.at[1, b], {"ra": prv})

    def ra_up(b):
        return remote(edge_hi.at[b], z_before.at[b], s_ra.at[0, b], r_ra.at[0, b], {"ra": nxt})

    def ra_dn(b):
        return remote(edge_lo.at[b], z_after.at[b], s_ra.at[1, b], r_ra.at[1, b], {"ra": prv})

    def to_twin(k, b):
        mine, other = ((mine_ed, other_ed), (mine_in, other_in))[k]
        return remote(mine.at[b], other.at[b], s_band.at[k, b], r_band.at[k, b], twin)

    has_hi, has_lo = dec < n_dec - 1, dec > 0
    lanes = iota((1, 1, cols), 2)
    inner = rows - 2 * RMAX
    order = [*range(RMAX), *range(rows - RMAX, rows), *range(RMAX, rows - RMAX)]

    def send_sky(b):
        sky_up(b).start()
        sky_dn(b).start()

    for_blocks(send_sky, late)

    def load_block(b):
        at = pl.multiple_of(b * CB, CB)
        block = sky_ref[:, pl.ds(at, CB), :].astype(jnp.float32)
        xs[0:rows * CB, :] = block.reshape(rows * CB, cols)

    def packed(read, count, deep, first):
        result = jnp.zeros((deep, CB, cols), jnp.float32)
        for g in range(-(-count // deep)):
            end = min(count, (g + 1) * deep)
            part = read(g * deep, end).astype(jnp.float32)
            if end < (g + 1) * deep:
                fill = jnp.zeros(((g + 1) * deep - end, CB, cols), jnp.float32)
                part = jnp.concatenate([part, fill], axis=0)
            turned = pltpu.roll(part, (WIDE * g - first) % cols, 2)
            inside = (lanes >= WIDE * g) & (lanes < WIDE * (g + 1))
            result = jnp.where(inside, turned, result)
        return result.astype(jnp.bfloat16)

    def pack_block(b):
        load_sky(b).wait()
        at = pl.multiple_of(b * CB, CB)

        def read(first, last):
            return sky_ref[first:last, pl.ds(at, CB), :]

        @pl.when(has_hi)
        def _():
            pack_up[b] = packed(read, rows, per, cols - WIDE)
            dec_up(b).start()

        @pl.when(has_lo)
        def _():
            pack_dn[b] = packed(read, rows, per, 0)
            dec_dn(b).start()

    def pack_far(j):
        b = late + j
        sky_up(b).wait_recv()
        sky_dn(b).wait_recv()

        def read(first, last):
            both = []
            if first < RMAX:
                both.append(z_before[b, first:min(last, RMAX)])
            if last > RMAX:
                both.append(z_after[b, max(first, RMAX) - RMAX:last - RMAX])
            return jnp.concatenate(both, axis=0)

        @pl.when(has_hi)
        def _():
            far_up[j] = packed(read, 2 * RMAX, far_per, cols - WIDE)
            far_dec_up(j).start()

        @pl.when(has_lo)
        def _():
            far_dn[j] = packed(read, 2 * RMAX, far_per, 0)
            far_dec_dn(j).start()

    ahead = min(2, blocks)
    for b in range(ahead):
        pack_block(jnp.int32(b))

    lax.fori_loop(1, RMAX + 1, table, 0)
    spare = xs.shape[0] - rows * CB
    xs[rows * CB:, :] = jnp.zeros((spare, cols), jnp.float32)
    if n_dec == 1:
        hs[...] = jnp.zeros_like(hs)
    load_radii.wait()
    load_valid.wait()
    weights = valid_ref[...].astype(jnp.float32)
    for at, x in enumerate(order):
        vb[at] = jnp.broadcast_to(weights[x:x + 1, :], (CB, cols)).astype(jnp.bfloat16)

    def unpack(low_ref, high_ref, deep, side):
        low = None if side == "high" else low_ref[...].astype(jnp.float32)
        high = None if side == "low" else high_ref[...].astype(jnp.float32)
        for g in range(groups):
            if side != "high":
                left = pltpu.roll(low, (cols - WIDE - WIDE * g) % cols, 2)
            if side != "low":
                right = pltpu.roll(high, (-WIDE * g) % cols, 2)
            on_right = lanes < cols // 2
            if side == "both":
                both = jnp.where(on_right, right, left)
            elif side == "low":
                both = jnp.where(on_right, 0.0, left)
            else:
                both = jnp.where(on_right, right, 0.0)
            hs[g * deep * CB:(g + 1) * deep * CB, :] = both.reshape(deep * CB, cols)

    def unpack_sides(low_ref, high_ref, deep):
        pl.when(has_lo & has_hi)(lambda: unpack(low_ref, high_ref, deep, "both"))
        pl.when(has_lo & jnp.logical_not(has_hi))(lambda: unpack(low_ref, high_ref, deep, "low"))
        pl.when(has_hi & jnp.logical_not(has_lo))(lambda: unpack(low_ref, high_ref, deep, "high"))

    def smooth_columns(b, height, put):
        for c in range(CB):
            rr = radii_ref[b * CB + c]
            main = xs[pl.ds(c, height, stride=CB), :]
            side = hs[pl.ds(c, height, stride=CB), :]
            left_hand = jnp.concatenate([main, side], axis=1).astype(jnp.bfloat16)
            part = jnp.dot(left_hand, tab_dec[rr], preferred_element_type=jnp.float32)
            put(c, part.astype(jnp.bfloat16).astype(jnp.float32))

    def smooth_rows(b, tab, height):
        for c in range(CB):
            rr = radii_ref[b * CB + c]
            column = ps[b, pl.ds(c, ext, stride=CB), :].astype(jnp.bfloat16)
            os[pl.ds(c, height, stride=CB), :] = jnp.dot(
                tab[rr], column, preferred_element_type=jnp.float32
            )

    def gram_of(mine, other, first, height):
        steps = next(n for n in (8, 6, 4, 2, 1) if height % n == 0)
        if height % 34 == 0:
            steps = 34
        if height % 22 == 0:
            steps = 22

        def gram(i, carry):
            def row(ref, x):
                return ref[:, pl.ds(x, 1), :, :].reshape(chans, cols)

            own = jnp.concatenate([row(mine, i * steps + s) for s in range(steps)], axis=1)
            oth = jnp.concatenate([row(other, i * steps + s) for s in range(steps)], axis=1)
            msk = jnp.concatenate([vb[first + i * steps + s] for s in range(steps)], axis=1)
            acc[...] += lax.dot_general(
                jnp.concatenate([own, msk], axis=0), jnp.concatenate([own, oth], axis=0),
                (((1,), (1,)), ((), ())), preferred_element_type=jnp.float32,
            )
            return carry

        lax.fori_loop(0, height // steps, gram, 0)

    def dec_block(b, carry):
        @pl.when(b + ahead < blocks)
        def _():
            pack_block(b + ahead)

        load_block(b)
        ps[b, rows8 * CB:ext * CB, :] = jnp.zeros(((ext - rows8) * CB, cols), jnp.float32)

        pl.when(has_lo)(lambda: dec_up(b).wait_recv())
        pl.when(has_hi)(lambda: dec_dn(b).wait_recv())
        unpack_sides(halo_lo.at[b], halo_hi.at[b], per)

        def put(c, part):
            ps[b, pl.ds(c, rows8, stride=CB), :] = part

        smooth_columns(b, rows8, put)

        @pl.when(b < late)
        def _():
            edge_lo[b] = ps[b, 0:RMAX * CB, :].reshape(RMAX, CB, cols).astype(jnp.bfloat16)
            last = ps[b, (rows - RMAX) * CB:rows * CB, :]
            edge_hi[b] = last.reshape(RMAX, CB, cols).astype(jnp.bfloat16)
            ra_up(b).start()
            ra_dn(b).start()

        smooth_rows(b, tab_in, in_rows)
        at = RMAX - in_at
        smooth = os[at * CB:(at + inner) * CB, :].reshape(inner, CB, cols).astype(jnp.bfloat16)
        out_ref[RMAX:rows - RMAX, pl.ds(pl.multiple_of(b * CB, CB), CB), :] = smooth
        mine_in[b] = smooth * vb[2 * RMAX:rows]
        to_twin(1, b).start()
        pl.when(b == late // 2)(lambda: for_blocks(pack_far, 0, blocks - late))
        return carry

    lax.fori_loop(0, blocks, dec_block, 0)

    def far_block(j):
        b = late + j
        for first, ref in ((0, z_before), (RMAX, z_after)):
            rim = ref[b].astype(jnp.float32)
            xs[first * CB:(first + RMAX) * CB, :] = rim.reshape(RMAX * CB, cols)
        pl.when(has_lo)(lambda: far_dec_up(j).wait_recv())
        pl.when(has_hi)(lambda: far_dec_dn(j).wait_recv())
        unpack_sides(far_lo.at[j], far_hi.at[j], far_per)
        height = up(2 * RMAX, 16)

        def put(c, part):
            os[pl.ds(c, height, stride=CB), :] = part

        smooth_columns(b, height, put)
        ps[b, (ext - RMAX) * CB:ext * CB, :] = os[0:RMAX * CB, :]
        ps[b, rows * CB:(rows + RMAX) * CB, :] = os[RMAX * CB:2 * RMAX * CB, :]

    for_blocks(far_block, 0, blocks - late)
    for_blocks(lambda b: to_twin(1, b).wait_recv())
    acc[...] = jnp.zeros_like(acc)
    gram_of(mine_in, other_in, 2 * RMAX, inner)

    def ra_block(i, carry):
        b = lax.rem(i + late, blocks)

        @pl.when(b < late)
        def _():
            ra_up(b).wait_recv()
            ra_dn(b).wait_recv()
            before = z_before[b].astype(jnp.float32)
            ps[b, (ext - RMAX) * CB:ext * CB, :] = before.reshape(RMAX * CB, cols)
            after = z_after[b].astype(jnp.float32)
            ps[b, rows * CB:(rows + RMAX) * CB, :] = after.reshape(RMAX * CB, cols)

        smooth_rows(b, tab_ed, 2 * edge_rows)
        low = os[0:RMAX * CB, :].reshape(RMAX, CB, cols).astype(jnp.bfloat16)
        at = 2 * edge_rows - rows8 + rows - RMAX
        high = os[at * CB:(at + RMAX) * CB, :].reshape(RMAX, CB, cols).astype(jnp.bfloat16)
        here = pl.ds(pl.multiple_of(b * CB, CB), CB)
        out_ref[0:RMAX, here, :] = low
        out_ref[rows - RMAX:rows, here, :] = high
        mine_ed[b, 0:RMAX] = low * vb[0:RMAX]
        mine_ed[b, RMAX:2 * RMAX] = high * vb[RMAX:2 * RMAX]
        to_twin(0, b).start()
        return carry

    lax.fori_loop(0, blocks, ra_block, 0)
    for_blocks(lambda b: to_twin(0, b).wait_recv())
    gram_of(mine_ed, other_ed, 0, 2 * RMAX)
    count = jnp.sum(weights, keepdims=True)
    aux[...] = jnp.where(iota((8, 2 * chans), 0) == 0, acc[chans:chans + 8, :], count)

    def part_of(p):
        return acc.at[pl.ds(pl.multiple_of(p * share, share), share), :]

    def rs(p, slot):
        return remote(part_of(p), shares.at[slot], s_rs.at[p], r_rs.at[slot], peer_id(p))

    def ag(p, slot):
        mypart = total.at[pl.ds(pl.multiple_of(slot * share, share), share), :]
        return remote(mypart, mypart, s_ag.at[p], r_ag.at[slot], peer_id(p))

    def au(p, slot):
        return remote(aux, aux_all.at[slot], s_aux.at[p], r_aux.at[slot], peer_id(p))

    def reducing(p, body):
        if reducers == peers:
            body()
        else:
            pl.when(p < reducers)(body)

    each_peer(lambda p: reducing(p, lambda: rs(p, rank).start()))
    each_peer(lambda p: au(p, rank).start())
    aux_all[rank] = aux[...]

    def reduce_own():
        shares[rank] = acc[pl.ds(pl.multiple_of(rank * share, share), share), :]
        each_peer(lambda p: rs(rank, p).wait_recv())
        whole = shares[0]
        whole = lax.fori_loop(1, peers, lambda p, t: t + shares[p], whole)
        total[pl.ds(pl.multiple_of(rank * share, share), share), :] = whole
        each_peer(lambda p: ag(p, rank).start())

    reducing(rank, reduce_own)
    each_peer(lambda p: au(p, p).wait_recv())
    sums = lax.fori_loop(1, peers, lambda p, t: t + aux_all[p], aux_all[0])
    count = sums[1:2, 0:1]
    means = sums[0:1, :] / count
    mean_ref[...] = means[:, 0:chans]
    column = jnp.transpose(jnp.broadcast_to(means[:, 0:chans], (chans, chans)))
    each_peer(lambda p: reducing(p, lambda: ag(p, p).wait_recv()))
    for k in range(2):
        across = means[:, k * chans:(k + 1) * chans]
        block = (total[:, k * chans:(k + 1) * chans] - count * column * across) / (count - 1.0)
        place = band if k == 0 else 1 - band
        cov_ref[pl.ds(pl.multiple_of(place * chans, chans), chans), :] = jnp.transpose(block)

    def finish(b):
        pl.when(has_hi)(lambda: dec_up(b).wait_send())
        pl.when(has_lo)(lambda: dec_dn(b).wait_send())
        to_twin(0, b).wait_send()
        to_twin(1, b).wait_send()

    def finish_late(b):
        ra_up(b).wait_send()
        ra_dn(b).wait_send()

    def finish_early(j):
        sky_up(late + j).wait_send()
        sky_dn(late + j).wait_send()
        pl.when(has_hi)(lambda: far_dec_up(j).wait_send())
        pl.when(has_lo)(lambda: far_dec_dn(j).wait_send())

    for_blocks(finish)
    for_blocks(finish_late, 0, late)
    for_blocks(finish_early, 0, blocks - late)
    each_peer(lambda p: reducing(p, lambda: rs(p, rank).wait_send()))
    each_peer(lambda p: au(p, rank).wait_send())
    reducing(rank, lambda: each_peer(lambda p: ag(p, rank).wait_send()))


def per_device(n_ra, n_dec, sky_maps, radii, valid):
    chans, rows, cols = sky_maps.shape
    blocks = chans // CB
    rows8 = up(rows, 16)
    groups = cols // WIDE
    per = -(-rows // groups)
    peers = n_ra * n_dec
    share = chans // min(peers, chans // 8)
    early = early_blocks(blocks)
    far_per = -(-2 * RMAX // groups)
    tall = max(per * groups, rows8)
    f32, b16, dma = jnp.float32, jnp.bfloat16, pltpu.SemaphoreType.DMA
    vmem = pl.BlockSpec(memory_space=pltpu.VMEM)
    hbm = pl.BlockSpec(memory_space=pltpu.HBM)
    in_at, in_rows, edge_rows = inner_rows(rows)
    inner, outer = rows - 2 * RMAX, 2 * RMAX
    flat = jnp.transpose(sky_maps, (1, 0, 2))
    packed = pltpu.VMEM((blocks, per, CB, cols), b16)
    far = pltpu.VMEM((early, far_per, CB, cols), b16)
    edge = pltpu.VMEM((blocks, RMAX, CB, cols), b16)
    smoothed, mean, cov = pl.pallas_call(
        functools.partial(kernel, (n_ra, n_dec, rows, chans, cols)),
        out_shape=(
            jax.ShapeDtypeStruct((rows, chans, cols), b16),
            jax.ShapeDtypeStruct((1, chans), f32),
            jax.ShapeDtypeStruct((2 * chans, chans), f32),
        ),
        in_specs=[hbm, hbm, hbm],
        out_specs=(vmem, vmem, vmem),
        scratch_shapes=[
            pltpu.VMEM((rows, chans, cols), b16),
            pltpu.VMEM((rows, cols), jnp.int32),
            pltpu.SMEM((chans,), jnp.int32),
            dma((blocks + 2,)),
            pltpu.VMEM((RMAX + 1, 2 * cols, cols), b16),
            pltpu.VMEM((RMAX + 1, in_rows, 128), b16),
            pltpu.VMEM((RMAX + 1, 2 * edge_rows, 128), b16),
            pltpu.VMEM((tall * CB, cols), f32),
            pltpu.VMEM((tall * CB, cols), f32),
            pltpu.VMEM((rows8 * CB, cols), f32),
            pltpu.VMEM((blocks, 128 * CB, cols), f32),
            pltpu.VMEM((rows, CB, cols), b16),
            pltpu.VMEM((blocks, inner, CB, cols), b16),
            pltpu.VMEM((blocks, outer, CB, cols), b16),
            pltpu.VMEM((blocks, inner, CB, cols), b16),
            pltpu.VMEM((blocks, outer, CB, cols), b16),
            packed, packed, packed, packed,
            far, far, far, far,
            edge, edge, edge, edge,
            pltpu.VMEM((chans + CB, 2 * chans), f32),
            pltpu.VMEM((peers, share, 2 * chans), f32),
            pltpu.VMEM((chans, 2 * chans), f32),
            pltpu.VMEM((8, 2 * chans), f32),
            pltpu.VMEM((peers, 8, 2 * chans), f32),
            dma((2, blocks + early)), dma((2, blocks + early)),
            dma((2, blocks)), dma((2, blocks)), dma((2, blocks)), dma((2, blocks)),
            dma((peers,)), dma((peers,)), dma((peers,)), dma((peers,)), dma((peers,)), dma((peers,)),
        ],
        compiler_params=pltpu.CompilerParams(
            collective_id=0, has_side_effects=True, vmem_limit_bytes=60 * 1024 * 1024
        ),
    )(radii, flat, valid)
    return (jnp.transpose(smoothed, (1, 0, 2)), mean.reshape(chans), cov)


def solution(mesh):
    return jax.shard_map(
        functools.partial(per_device, mesh.shape["ra"], mesh.shape["dec"]),
        mesh=mesh,
        in_specs=(
            P(("groups", "band"), "ra", "dec"),
            P(("groups", "band")),
            P(("groups", "ra"), "dec"),
        ),
        out_specs=(P(("groups", "band"), "ra", "dec"), P(("groups", "band")), P("groups", "band")),
        check_vma=False,
    )
```

```python
import functools

import jax
import jax.numpy as jnp
from jax import lax
from jax.experimental import pallas as pl
from jax.experimental.pallas import tpu as pltpu
from jax.sharding import PartitionSpec as P

RMAX = 17
WIDE = RMAX + 1
CB = 16
EARLY = 2
MESH = pl.DeviceIdType.MESH


def up(value, step):
    return -(-value // step) * step


def iota(shape, dim):
    return lax.broadcasted_iota(jnp.int32, shape, dim)


def early_blocks(blocks):
    return min(EARLY, blocks - 1)


def inner_rows(rows):
    first = RMAX // 16 * 16
    last = up(rows - RMAX, 16)
    return first, last - first, up(RMAX, 8)


def kernel(
    dims, radii_hbm, sky_hbm, valid_hbm, out_ref, mean_ref, cov_ref,
    sky_ref, valid_ref, radii_ref, loads,
    tab_dec, tab_in, tab_ed, xs, hs, os, ps, vb, mine_in, mine_ed, other_in, other_ed,
    pack_up, pack_dn, halo_lo, halo_hi, far_up, far_dn, far_lo, far_hi, edge_lo, edge_hi, z_before, z_after,
    acc, shares, total, aux, aux_all,
    s_dec, r_dec, s_ra, r_ra, s_band, r_band, s_rs, r_rs, s_ag, r_ag, s_aux, r_aux,
):
    n_ra, n_dec, rows, chans, cols = dims
    blocks = chans // CB
    rows8 = up(rows, 16)
    groups = cols // WIDE
    per = -(-rows // groups)
    far_per = -(-2 * RMAX // groups)
    late = blocks - early_blocks(blocks)
    peers = n_ra * n_dec
    reducers = min(peers, chans // 8)
    share = chans // reducers
    ext = 128
    in_at, in_rows, edge_rows = inner_rows(rows)
    ra, dec, band = lax.axis_index("ra"), lax.axis_index("dec"), lax.axis_index("band")
    rank = ra * n_dec + dec
    nxt, prv = lax.rem(ra + 1, n_ra), lax.rem(ra + n_ra - 1, n_ra)
    twin = {"band": 1 - band}

    def peer_id(p):
        return {"ra": p // n_dec, "dec": lax.rem(p, n_dec)}

    def each_peer(body):
        def step(d, carry):
            body(lax.rem(rank + d, peers))
            return carry
        lax.fori_loop(1, peers, step, 0)

    def table(r, carry):
        radius = r.astype(jnp.float32)
        spread = 0.5 * radius
        k = lax.rem(iota((8, cols), 0) - iota((8, cols), 1) + cols + cols // 2, cols) - cols // 2
        k = k.astype(jnp.float32)
        raw = jnp.where(jnp.abs(k) <= radius, jnp.exp(-(k * k) / (2.0 * spread * spread)), 0.0)
        first = raw / jnp.sum(raw, axis=1, keepdims=True)
        full = jnp.concatenate([pltpu.roll(first, 8 * t, 1) for t in range(cols // 8)], axis=0)
        near = jnp.abs(iota((cols, cols), 0) - iota((cols, cols), 1)) <= cols // 2
        tab_in[r] = full[in_at:in_at + in_rows].astype(jnp.bfloat16)
        ends = jnp.concatenate([full[0:edge_rows], full[rows8 - edge_rows:rows8]], axis=0)
        tab_ed[r] = ends.astype(jnp.bfloat16)
        tab_dec[r, 0:cols, :] = jnp.where(near, full, 0.0).astype(jnp.bfloat16)
        tab_dec[r, cols:2 * cols, :] = jnp.where(near, 0.0, full).astype(jnp.bfloat16)
        return carry

    def load_sky(b):
        at = pl.multiple_of(b * CB, CB)
        return pltpu.make_async_copy(
            sky_hbm.at[:, pl.ds(at, CB), :], sky_ref.at[:, pl.ds(at, CB), :], loads.at[b]
        )

    load_valid = pltpu.make_async_copy(valid_hbm, valid_ref, loads.at[blocks])
    load_radii = pltpu.make_async_copy(radii_hbm, radii_ref, loads.at[blocks + 1])
    barrier = pltpu.get_barrier_semaphore()
    each_peer(lambda p: pl.semaphore_signal(barrier, inc=1, device_id=peer_id(p), device_id_type=MESH))
    pl.semaphore_signal(barrier, inc=1, device_id=twin, device_id_type=MESH)

    def for_blocks(body, first=0, last=blocks):
        def step(b, carry):
            body(b)
            return carry
        lax.fori_loop(first, last, step, 0)

    for_blocks(lambda b: load_sky(b).start())
    load_valid.start()
    load_radii.start()
    pl.semaphore_wait(barrier, peers)

    def remote(src, dst, send, recv, target):
        return pltpu.make_async_remote_copy(
            src_ref=src, dst_ref=dst, send_sem=send, recv_sem=recv, device_id=target, device_id_type=MESH
        )

    def dec_up(b):
        return remote(pack_up.at[b], halo_lo.at[b], s_dec.at[0, b], r_dec.at[0, b], {"dec": dec + 1})

    def dec_dn(b):
        return remote(pack_dn.at[b], halo_hi.at[b], s_dec.at[1, b], r_dec.at[1, b], {"dec": dec - 1})

    def far_dec_up(j):
        return remote(
            far_up.at[j], far_lo.at[j], s_dec.at[0, blocks + j], r_dec.at[0, blocks + j], {"dec": dec + 1}
        )

    def far_dec_dn(j):
        return remote(
            far_dn.at[j], far_hi.at[j], s_dec.at[1, blocks + j], r_dec.at[1, blocks + j], {"dec": dec - 1}
        )

    def sky_up(b):
        rim = sky_hbm.at[pl.ds(rows - RMAX, RMAX), pl.ds(pl.multiple_of(b * CB, CB), CB), :]
        return remote(rim, z_before.at[b], s_ra.at[0, b], r_ra.at[0, b], {"ra": nxt})

    def sky_dn(b):
        rim = sky_hbm.at[pl.ds(0, RMAX), pl.ds(pl.multiple_of(b * CB, CB), CB), :]
        return remote(rim, z_after.at[b], s_ra.at[1, b], r_ra.at[1, b], {"ra": prv})

    def ra_up(b):
        return remote(edge_hi.at[b], z_before.at[b], s_ra.at[0, b], r_ra.at[0, b], {"ra": nxt})

    def ra_dn(b):
        return remote(edge_lo.at[b], z_after.at[b], s_ra.at[1, b], r_ra.at[1, b], {"ra": prv})

    def to_twin(k, b):
        mine, other = ((mine_ed, other_ed), (mine_in, other_in))[k]
        return remote(mine.at[b], other.at[b], s_band.at[k, b], r_band.at[k, b], twin)

    has_hi, has_lo = dec < n_dec - 1, dec > 0
    lanes = iota((1, 1, cols), 2)
    inner = rows - 2 * RMAX
    order = [*range(RMAX), *range(rows - RMAX, rows), *range(RMAX, rows - RMAX)]

    def send_sky(b):
        sky_up(b).start()
        sky_dn(b).start()

    for_blocks(send_sky, late)

    def load_block(b):
        at = pl.multiple_of(b * CB, CB)
        block = sky_ref[:, pl.ds(at, CB), :].astype(jnp.float32)
        xs[0:rows * CB, :] = block.reshape(rows * CB, cols)

    def packed(read, count, deep, first):
        result = jnp.zeros((deep, CB, cols), jnp.float32)
        for g in range(-(-count // deep)):
            end = min(count, (g + 1) * deep)
            part = read(g * deep, end).astype(jnp.float32)
            if end < (g + 1) * deep:
                fill = jnp.zeros(((g + 1) * deep - end, CB, cols), jnp.float32)
                part = jnp.concatenate([part, fill], axis=0)
            turned = pltpu.roll(part, (WIDE * g - first) % cols, 2)
            inside = (lanes >= WIDE * g) & (lanes < WIDE * (g + 1))
            result = jnp.where(inside, turned, result)
        return result.astype(jnp.bfloat16)

    def pack_block(b):
        load_sky(b).wait()
        at = pl.multiple_of(b * CB, CB)

        def read(first, last):
            return sky_ref[first:last, pl.ds(at, CB), :]

        @pl.when(has_hi)
        def _():
            pack_up[b] = packed(read, rows, per, cols - WIDE)
            dec_up(b).start()

        @pl.when(has_lo)
        def _():
            pack_dn[b] = packed(read, rows, per, 0)
            dec_dn(b).start()

    def pack_far(j):
        b = late + j
        sky_up(b).wait_recv()
        sky_dn(b).wait_recv()

        def read(first, last):
            both = []
            if first < RMAX:
                both.append(z_before[b, first:min(last, RMAX)])
            if last > RMAX:
                both.append(z_after[b, max(first, RMAX) - RMAX:last - RMAX])
            return jnp.concatenate(both, axis=0)

        @pl.when(has_hi)
        def _():
            far_up[j] = packed(read, 2 * RMAX, far_per, cols - WIDE)
            far_dec_up(j).start()

        @pl.when(has_lo)
        def _():
            far_dn[j] = packed(read, 2 * RMAX, far_per, 0)
            far_dec_dn(j).start()

    ahead = min(2, blocks)
    for b in range(ahead):
        pack_block(jnp.int32(b))

    lax.fori_loop(1, RMAX + 1, table, 0)
    spare = xs.shape[0] - rows * CB
    xs[rows * CB:, :] = jnp.zeros((spare, cols), jnp.float32)
    if n_dec == 1:
        hs[...] = jnp.zeros_like(hs)
    load_radii.wait()
    load_valid.wait()
    weights = valid_ref[...].astype(jnp.float32)
    for at, x in enumerate(order):
        vb[at] = jnp.broadcast_to(weights[x:x + 1, :], (CB, cols)).astype(jnp.bfloat16)

    def unpack(low_ref, high_ref, deep, side):
        low = None if side == "high" else low_ref[...].astype(jnp.float32)
        high = None if side == "low" else high_ref[...].astype(jnp.float32)
        for g in range(groups):
            if side != "high":
                left = pltpu.roll(low, (cols - WIDE - WIDE * g) % cols, 2)
            if side != "low":
                right = pltpu.roll(high, (-WIDE * g) % cols, 2)
            on_right = lanes < cols // 2
            if side == "both":
                both = jnp.where(on_right, right, left)
            elif side == "low":
                both = jnp.where(on_right, 0.0, left)
            else:
                both = jnp.where(on_right, right, 0.0)
            hs[g * deep * CB:(g + 1) * deep * CB, :] = both.reshape(deep * CB, cols)

    def unpack_sides(low_ref, high_ref, deep):
        pl.when(has_lo & has_hi)(lambda: unpack(low_ref, high_ref, deep, "both"))
        pl.when(has_lo & jnp.logical_not(has_hi))(lambda: unpack(low_ref, high_ref, deep, "low"))
        pl.when(has_hi & jnp.logical_not(has_lo))(lambda: unpack(low_ref, high_ref, deep, "high"))

    def smooth_columns(b, height, put):
        for c in range(CB):
            rr = radii_ref[b * CB + c]
            main = xs[pl.ds(c, height, stride=CB), :]
            side = hs[pl.ds(c, height, stride=CB), :]
            left_hand = jnp.concatenate([main, side], axis=1).astype(jnp.bfloat16)
            part = jnp.dot(left_hand, tab_dec[rr], preferred_element_type=jnp.float32)
            put(c, part.astype(jnp.bfloat16).astype(jnp.float32))

    def smooth_rows(b, tab, height):
        for c in range(CB):
            rr = radii_ref[b * CB + c]
            column = ps[b, pl.ds(c, ext, stride=CB), :].astype(jnp.bfloat16)
            os[pl.ds(c, height, stride=CB), :] = jnp.dot(
                tab[rr], column, preferred_element_type=jnp.float32
            )

    def gram_of(mine, other, first, height):
        steps = next(n for n in (8, 6, 4, 2, 1) if height % n == 0)
        if height % 34 == 0:
            steps = 34
        if height % 22 == 0:
            steps = 22

        def gram(i, carry):
            def row(ref, x):
                return ref[:, pl.ds(x, 1), :, :].reshape(chans, cols)

            own = jnp.concatenate([row(mine, i * steps + s) for s in range(steps)], axis=1)
            oth = jnp.concatenate([row(other, i * steps + s) for s in range(steps)], axis=1)
            msk = jnp.concatenate([vb[first + i * steps + s] for s in range(steps)], axis=1)
            acc[...] += lax.dot_general(
                jnp.concatenate([own, msk], axis=0), jnp.concatenate([own, oth], axis=0),
                (((1,), (1,)), ((), ())), preferred_element_type=jnp.float32,
            )
            return carry

        lax.fori_loop(0, height // steps, gram, 0)

    def dec_block(b, carry):
        @pl.when(b + ahead < blocks)
        def _():
            pack_block(b + ahead)

        load_block(b)
        ps[b, rows8 * CB:ext * CB, :] = jnp.zeros(((ext - rows8) * CB, cols), jnp.float32)

        pl.when(has_lo)(lambda: dec_up(b).wait_recv())
        pl.when(has_hi)(lambda: dec_dn(b).wait_recv())
        unpack_sides(halo_lo.at[b], halo_hi.at[b], per)

        def put(c, part):
            ps[b, pl.ds(c, rows8, stride=CB), :] = part

        smooth_columns(b, rows8, put)

        @pl.when(b < late)
        def _():
            edge_lo[b] = ps[b, 0:RMAX * CB, :].reshape(RMAX, CB, cols).astype(jnp.bfloat16)
            last = ps[b, (rows - RMAX) * CB:rows * CB, :]
            edge_hi[b] = last.reshape(RMAX, CB, cols).astype(jnp.bfloat16)
            ra_up(b).start()
            ra_dn(b).start()

        smooth_rows(b, tab_in, in_rows)
        at = RMAX - in_at
        smooth = os[at * CB:(at + inner) * CB, :].reshape(inner, CB, cols).astype(jnp.bfloat16)
        out_ref[RMAX:rows - RMAX, pl.ds(pl.multiple_of(b * CB, CB), CB), :] = smooth
        mine_in[b] = smooth * vb[2 * RMAX:rows]
        to_twin(1, b).start()
        pl.when(b == late // 2)(lambda: for_blocks(pack_far, 0, blocks - late))
        return carry

    lax.fori_loop(0, blocks, dec_block, 0)

    def far_block(j):
        b = late + j
        for first, ref in ((0, z_before), (RMAX, z_after)):
            rim = ref[b].astype(jnp.float32)
            xs[first * CB:(first + RMAX) * CB, :] = rim.reshape(RMAX * CB, cols)
        pl.when(has_lo)(lambda: far_dec_up(j).wait_recv())
        pl.when(has_hi)(lambda: far_dec_dn(j).wait_recv())
        unpack_sides(far_lo.at[j], far_hi.at[j], far_per)
        height = up(2 * RMAX, 16)

        def put(c, part):
            os[pl.ds(c, height, stride=CB), :] = part

        smooth_columns(b, height, put)
        ps[b, (ext - RMAX) * CB:ext * CB, :] = os[0:RMAX * CB, :]
        ps[b, rows * CB:(rows + RMAX) * CB, :] = os[RMAX * CB:2 * RMAX * CB, :]

    for_blocks(far_block, 0, blocks - late)
    for_blocks(lambda b: to_twin(1, b).wait_recv())
    acc[...] = jnp.zeros_like(acc)
    gram_of(mine_in, other_in, 2 * RMAX, inner)

    def ra_block(i, carry):
        b = lax.rem(i + late, blocks)

        @pl.when(b < late)
        def _():
            ra_up(b).wait_recv()
            ra_dn(b).wait_recv()
            before = z_before[b].astype(jnp.float32)
            ps[b, (ext - RMAX) * CB:ext * CB, :] = before.reshape(RMAX * CB, cols)
            after = z_after[b].astype(jnp.float32)
            ps[b, rows * CB:(rows + RMAX) * CB, :] = after.reshape(RMAX * CB, cols)

        smooth_rows(b, tab_ed, 2 * edge_rows)
        low = os[0:RMAX * CB, :].reshape(RMAX, CB, cols).astype(jnp.bfloat16)
        at = 2 * edge_rows - rows8 + rows - RMAX
        high = os[at * CB:(at + RMAX) * CB, :].reshape(RMAX, CB, cols).astype(jnp.bfloat16)
        here = pl.ds(pl.multiple_of(b * CB, CB), CB)
        out_ref[0:RMAX, here, :] = low
        out_ref[rows - RMAX:rows, here, :] = high
        mine_ed[b, 0:RMAX] = low * vb[0:RMAX]
        mine_ed[b, RMAX:2 * RMAX] = high * vb[RMAX:2 * RMAX]
        to_twin(0, b).start()
        return carry

    lax.fori_loop(0, blocks, ra_block, 0)
    for_blocks(lambda b: to_twin(0, b).wait_recv())
    gram_of(mine_ed, other_ed, 0, 2 * RMAX)
    count = jnp.sum(weights, keepdims=True)
    aux[...] = jnp.where(iota((8, 2 * chans), 0) == 0, acc[chans:chans + 8, :], count)

    def part_of(p):
        return acc.at[pl.ds(pl.multiple_of(p * share, share), share), :]

    def rs(p, slot):
        return remote(part_of(p), shares.at[slot], s_rs.at[p], r_rs.at[slot], peer_id(p))

    def ag(p, slot):
        mypart = total.at[pl.ds(pl.multiple_of(slot * share, share), share), :]
        return remote(mypart, mypart, s_ag.at[p], r_ag.at[slot], peer_id(p))

    def au(p, slot):
        return remote(aux, aux_all.at[slot], s_aux.at[p], r_aux.at[slot], peer_id(p))

    def reducing(p, body):
        if reducers == peers:
            body()
        else:
            pl.when(p < reducers)(body)

    each_peer(lambda p: reducing(p, lambda: rs(p, rank).start()))
    each_peer(lambda p: au(p, rank).start())
    aux_all[rank] = aux[...]

    def reduce_own():
        shares[rank] = acc[pl.ds(pl.multiple_of(rank * share, share), share), :]
        each_peer(lambda p: rs(rank, p).wait_recv())
        whole = shares[0]
        whole = lax.fori_loop(1, peers, lambda p, t: t + shares[p], whole)
        total[pl.ds(pl.multiple_of(rank * share, share), share), :] = whole
        each_peer(lambda p: ag(p, rank).start())

    reducing(rank, reduce_own)
    each_peer(lambda p: au(p, p).wait_recv())
    sums = lax.fori_loop(1, peers, lambda p, t: t + aux_all[p], aux_all[0])
    count = sums[1:2, 0:1]
    means = sums[0:1, :] / count
    mean_ref[...] = means[:, 0:chans]
    column = jnp.transpose(jnp.broadcast_to(means[:, 0:chans], (chans, chans)))
    each_peer(lambda p: reducing(p, lambda: ag(p, p).wait_recv()))
    for k in range(2):
        across = means[:, k * chans:(k + 1) * chans]
        block = (total[:, k * chans:(k + 1) * chans] - count * column * across) / (count - 1.0)
        place = band if k == 0 else 1 - band
        cov_ref[pl.ds(pl.multiple_of(place * chans, chans), chans), :] = jnp.transpose(block)

    def finish(b):
        pl.when(has_hi)(lambda: dec_up(b).wait_send())
        pl.when(has_lo)(lambda: dec_dn(b).wait_send())
        to_twin(0, b).wait_send()
        to_twin(1, b).wait_send()

    def finish_late(b):
        ra_up(b).wait_send()
        ra_dn(b).wait_send()

    def finish_early(j):
        sky_up(late + j).wait_send()
        sky_dn(late + j).wait_send()
        pl.when(has_hi)(lambda: far_dec_up(j).wait_send())
        pl.when(has_lo)(lambda: far_dec_dn(j).wait_send())

    for_blocks(finish)
    for_blocks(finish_late, 0, late)
    for_blocks(finish_early, 0, blocks - late)
    each_peer(lambda p: reducing(p, lambda: rs(p, rank).wait_send()))
    each_peer(lambda p: au(p, rank).wait_send())
    reducing(rank, lambda: each_peer(lambda p: ag(p, rank).wait_send()))


def store(smoothed_ref, mean_ref, cov_ref, smoothed_hbm, mean_hbm, cov_hbm, sems):
    pairs = ((smoothed_ref, smoothed_hbm), (mean_ref, mean_hbm), (cov_ref, cov_hbm))
    copies = [pltpu.make_async_copy(src, dst, sems.at[i]) for i, (src, dst) in enumerate(pairs)]
    for copy in copies:
        copy.start()
    for copy in copies:
        copy.wait()


def per_device(n_ra, n_dec, sky_maps, radii, valid):
    chans, rows, cols = sky_maps.shape
    blocks = chans // CB
    rows8 = up(rows, 16)
    groups = cols // WIDE
    per = -(-rows // groups)
    peers = n_ra * n_dec
    share = chans // min(peers, chans // 8)
    early = early_blocks(blocks)
    far_per = -(-2 * RMAX // groups)
    tall = max(per * groups, rows8)
    f32, b16, dma = jnp.float32, jnp.bfloat16, pltpu.SemaphoreType.DMA
    vmem = pl.BlockSpec(memory_space=pltpu.VMEM)
    hbm = pl.BlockSpec(memory_space=pltpu.HBM)
    in_at, in_rows, edge_rows = inner_rows(rows)
    inner, outer = rows - 2 * RMAX, 2 * RMAX
    flat = pltpu.with_memory_space_constraint(jnp.transpose(sky_maps, (1, 0, 2)), pltpu.HBM)
    radii = pltpu.with_memory_space_constraint(radii, pltpu.HBM)
    valid = pltpu.with_memory_space_constraint(valid, pltpu.HBM)
    packed = pltpu.VMEM((blocks, per, CB, cols), b16)
    far = pltpu.VMEM((early, far_per, CB, cols), b16)
    edge = pltpu.VMEM((blocks, RMAX, CB, cols), b16)
    smoothed, mean, cov = pl.pallas_call(
        functools.partial(kernel, (n_ra, n_dec, rows, chans, cols)),
        out_shape=(
            pltpu.VMEM((rows, chans, cols), b16),
            pltpu.VMEM((1, chans), f32),
            pltpu.VMEM((2 * chans, chans), f32),
        ),
        in_specs=[hbm, hbm, hbm],
        out_specs=(vmem, vmem, vmem),
        scratch_shapes=[
            pltpu.VMEM((rows, chans, cols), b16),
            pltpu.VMEM((rows, cols), jnp.int32),
            pltpu.SMEM((chans,), jnp.int32),
            dma((blocks + 2,)),
            pltpu.VMEM((RMAX + 1, 2 * cols, cols), b16),
            pltpu.VMEM((RMAX + 1, in_rows, 128), b16),
            pltpu.VMEM((RMAX + 1, 2 * edge_rows, 128), b16),
            pltpu.VMEM((tall * CB, cols), f32),
            pltpu.VMEM((tall * CB, cols), f32),
            pltpu.VMEM((rows8 * CB, cols), f32),
            pltpu.VMEM((blocks, 128 * CB, cols), f32),
            pltpu.VMEM((rows, CB, cols), b16),
            pltpu.VMEM((blocks, inner, CB, cols), b16),
            pltpu.VMEM((blocks, outer, CB, cols), b16),
            pltpu.VMEM((blocks, inner, CB, cols), b16),
            pltpu.VMEM((blocks, outer, CB, cols), b16),
            packed, packed, packed, packed,
            far, far, far, far,
            edge, edge, edge, edge,
            pltpu.VMEM((chans + CB, 2 * chans), f32),
            pltpu.VMEM((peers, share, 2 * chans), f32),
            pltpu.VMEM((chans, 2 * chans), f32),
            pltpu.VMEM((8, 2 * chans), f32),
            pltpu.VMEM((peers, 8, 2 * chans), f32),
            dma((2, blocks + early)), dma((2, blocks + early)),
            dma((2, blocks)), dma((2, blocks)), dma((2, blocks)), dma((2, blocks)),
            dma((peers,)), dma((peers,)), dma((peers,)), dma((peers,)), dma((peers,)), dma((peers,)),
        ],
        compiler_params=pltpu.CompilerParams(
            collective_id=0, has_side_effects=True, vmem_limit_bytes=40 * 1024 * 1024
        ),
    )(radii, flat, valid)
    smoothed, mean, cov = pl.pallas_call(
        store,
        out_shape=(
            jax.ShapeDtypeStruct((rows, chans, cols), b16),
            jax.ShapeDtypeStruct((1, chans), f32),
            jax.ShapeDtypeStruct((2 * chans, chans), f32),
        ),
        in_specs=(vmem, vmem, vmem),
        out_specs=(hbm, hbm, hbm),
        scratch_shapes=[dma((3,))],
    )(*(pltpu.with_memory_space_constraint(part, pltpu.VMEM) for part in (smoothed, mean, cov)))
    return (jnp.transpose(smoothed, (1, 0, 2)), mean.reshape(chans), cov)


def solution(mesh):
    return jax.shard_map(
        functools.partial(per_device, mesh.shape["ra"], mesh.shape["dec"]),
        mesh=mesh,
        in_specs=(
            P(("groups", "band"), "ra", "dec"),
            P(("groups", "band")),
            P(("groups", "ra"), "dec"),
        ),
        out_specs=(P(("groups", "band"), "ra", "dec"), P(("groups", "band")), P("groups", "band")),
        check_vma=False,
    )
```

```python
import functools

import jax
import jax.numpy as jnp
from jax import lax
from jax.experimental import pallas as pl
from jax.experimental.pallas import tpu as pltpu
from jax.sharding import PartitionSpec as P

RMAX = 17
WIDE = RMAX + 1
CB = 16
EARLY = 2
SINGLE = 2
TABLES_LESS = 6
MESH = pl.DeviceIdType.MESH


def up(value, step):
    return -(-value // step) * step


def iota(shape, dim):
    return lax.broadcasted_iota(jnp.int32, shape, dim)


def early_blocks(blocks):
    return min(EARLY, blocks - 1)


def inner_rows(rows):
    first = RMAX // 16 * 16
    last = up(rows - RMAX, 16)
    return first, last - first, up(RMAX, 8)


def kernel(
    dims, radii_hbm, sky_hbm, valid_hbm, out_ref, mean_ref, cov_ref,
    sky_ref, valid_ref, radii_ref, loads,
    tab_dec, tab_in, tab_ed, xs, hs, os, ps, vb, mine_in, mine_ed, other_in, other_ed,
    pack_up, pack_dn, halo_lo, halo_hi, far_up, far_dn, far_lo, far_hi, edge_lo, edge_hi, z_before, z_after,
    raw_before, raw_after,
    acc, shares, total, aux, aux_all,
    s_dec, r_dec, s_ra, r_ra, s_band, r_band, s_rs, r_rs, s_ag, r_ag, s_aux, r_aux,
):
    n_ra, n_dec, rows, chans, cols = dims
    blocks = chans // CB
    rows8 = up(rows, 16)
    groups = cols // WIDE
    per = -(-rows // groups)
    far_per = -(-2 * RMAX // groups)
    late = blocks - early_blocks(blocks)
    peers = n_ra * n_dec
    reducers = min(peers, chans // 8)
    share = chans // reducers
    ext = 128
    in_at, in_rows, edge_rows = inner_rows(rows)
    ra, dec, band = lax.axis_index("ra"), lax.axis_index("dec"), lax.axis_index("band")
    rank = ra * n_dec + dec
    nxt, prv = lax.rem(ra + 1, n_ra), lax.rem(ra + n_ra - 1, n_ra)
    twin = {"band": 1 - band}

    def peer_id(p):
        return {"ra": p // n_dec, "dec": lax.rem(p, n_dec)}

    def each_peer(body):
        if peers <= 8:
            for d in range(1, peers):
                body(lax.rem(rank + d, peers))
            return

        def step(d, carry):
            body(lax.rem(rank + d, peers))
            return carry
        lax.fori_loop(1, peers, step, 0)

    def table(r, carry):
        radius = r.astype(jnp.float32)
        spread = 0.5 * radius
        k = lax.rem(iota((8, cols), 0) - iota((8, cols), 1) + cols + cols // 2, cols) - cols // 2
        k = k.astype(jnp.float32)
        raw = jnp.where(jnp.abs(k) <= radius, jnp.exp(-(k * k) / (2.0 * spread * spread)), 0.0)
        first = raw / jnp.sum(raw, axis=1, keepdims=True)
        full = jnp.concatenate([pltpu.roll(first, 8 * t, 1) for t in range(cols // 8)], axis=0)
        near = jnp.abs(iota((cols, cols), 0) - iota((cols, cols), 1)) <= cols // 2
        tab_in[r] = full[in_at:in_at + in_rows].astype(jnp.bfloat16)
        ends = jnp.concatenate([full[0:edge_rows], full[rows8 - edge_rows:rows8]], axis=0)
        tab_ed[r] = ends.astype(jnp.bfloat16)
        tab_dec[r, 0:cols, :] = jnp.where(near, full, 0.0).astype(jnp.bfloat16)
        tab_dec[r, cols:2 * cols, :] = jnp.where(near, 0.0, full).astype(jnp.bfloat16)
        return carry

    def load_sky(b):
        at = pl.multiple_of(b * CB, CB)
        return pltpu.make_async_copy(
            sky_hbm.at[:, pl.ds(at, CB), :], sky_ref.at[:, pl.ds(at, CB), :], loads.at[b]
        )

    load_valid = pltpu.make_async_copy(valid_hbm, valid_ref, loads.at[blocks])
    load_radii = pltpu.make_async_copy(radii_hbm, radii_ref, loads.at[blocks + 1])
    barrier = pltpu.get_barrier_semaphore()
    each_peer(lambda p: pl.semaphore_signal(barrier, inc=1, device_id=peer_id(p), device_id_type=MESH))
    pl.semaphore_signal(barrier, inc=1, device_id=twin, device_id_type=MESH)

    def for_blocks(body, first=0, last=blocks):
        def step(b, carry):
            body(b)
            return carry
        lax.fori_loop(first, last, step, 0)


    def remote(src, dst, send, recv, target):
        return pltpu.make_async_remote_copy(
            src_ref=src, dst_ref=dst, send_sem=send, recv_sem=recv, device_id=target, device_id_type=MESH
        )

    def dec_up(b):
        return remote(pack_up.at[b], halo_lo.at[b], s_dec.at[0, b], r_dec.at[0, b], {"dec": dec + 1})

    def dec_dn(b):
        return remote(pack_dn.at[b], halo_hi.at[b], s_dec.at[1, b], r_dec.at[1, b], {"dec": dec - 1})

    def far_dec_up(j):
        return remote(
            far_up.at[j], far_lo.at[j], s_dec.at[0, blocks + j], r_dec.at[0, blocks + j], {"dec": dec + 1}
        )

    def far_dec_dn(j):
        return remote(
            far_dn.at[j], far_hi.at[j], s_dec.at[1, blocks + j], r_dec.at[1, blocks + j], {"dec": dec - 1}
        )

    def sky_up():
        rim = sky_hbm.at[pl.ds(rows - RMAX, RMAX), pl.ds(late * CB, chans - late * CB), :]
        return remote(rim, raw_before, s_ra.at[0, late], r_ra.at[0, late], {"ra": nxt})

    def sky_dn():
        rim = sky_hbm.at[pl.ds(0, RMAX), pl.ds(late * CB, chans - late * CB), :]
        return remote(rim, raw_after, s_ra.at[1, late], r_ra.at[1, late], {"ra": prv})

    def ra_up(b, n):
        part = pl.ds(b, n)
        return remote(edge_hi.at[part], z_before.at[part], s_ra.at[0, b], r_ra.at[0, b], {"ra": nxt})

    def ra_dn(b, n):
        part = pl.ds(b, n)
        return remote(edge_lo.at[part], z_after.at[part], s_ra.at[1, b], r_ra.at[1, b], {"ra": prv})

    def ra_both(b, n, body):
        body(ra_up(b, n))
        body(ra_dn(b, n))

    def to_twin(k, b):
        mine, other = ((mine_ed, other_ed), (mine_in, other_in))[k]
        return remote(mine.at[b], other.at[b], s_band.at[k, b], r_band.at[k, b], twin)

    has_hi, has_lo = dec < n_dec - 1, dec > 0
    lanes = iota((1, 1, cols), 2)
    inner = rows - 2 * RMAX
    order = [*range(RMAX), *range(rows - RMAX, rows), *range(RMAX, rows - RMAX)]

    def send_rims():
        @pl.when(ra == 0)
        def _():
            sky_dn().start()
            sky_up().start()

        @pl.when(ra > 0)
        def _():
            sky_up().start()
            sky_dn().start()

    def load_block(b):
        at = pl.multiple_of(b * CB, CB)
        block = sky_ref[:, pl.ds(at, CB), :].astype(jnp.float32)
        xs[0:rows * CB, :] = block.reshape(rows * CB, cols)

    def packed(read, count, deep, first):
        result = jnp.zeros((deep, CB, cols), jnp.float32)
        for g in range(-(-count // deep)):
            end = min(count, (g + 1) * deep)
            part = read(g * deep, end).astype(jnp.float32)
            if end < (g + 1) * deep:
                fill = jnp.zeros(((g + 1) * deep - end, CB, cols), jnp.float32)
                part = jnp.concatenate([part, fill], axis=0)
            turned = pltpu.roll(part, (WIDE * g - first) % cols, 2)
            inside = (lanes >= WIDE * g) & (lanes < WIDE * (g + 1))
            result = jnp.where(inside, turned, result)
        return result.astype(jnp.bfloat16)

    def pack_block(b):
        pack_only(b)
        send_packed(b)

    def send_packed(b):
        pl.when(has_hi)(lambda: dec_up(b).start())
        pl.when(has_lo)(lambda: dec_dn(b).start())

    def pack_only(b):
        load_sky(b).wait()
        at = pl.multiple_of(b * CB, CB)

        def read(first, last):
            return sky_ref[first:last, pl.ds(at, CB), :]

        @pl.when(has_hi)
        def _():
            pack_up[b] = packed(read, rows, per, cols - WIDE)

        @pl.when(has_lo)
        def _():
            pack_dn[b] = packed(read, rows, per, 0)

    def pack_far(j):
        here = pl.ds(pl.multiple_of(j * CB, CB), CB)

        def read(first, last):
            both = []
            if first < RMAX:
                both.append(raw_before[first:min(last, RMAX), here, :])
            if last > RMAX:
                both.append(raw_after[max(first, RMAX) - RMAX:last - RMAX, here, :])
            return jnp.concatenate(both, axis=0)

        @pl.when(has_hi)
        def _():
            far_up[j] = packed(read, 2 * RMAX, far_per, cols - WIDE)
            far_dec_up(j).start()

        @pl.when(has_lo)
        def _():
            far_dn[j] = packed(read, 2 * RMAX, far_per, 0)
            far_dec_dn(j).start()

    ahead = min(2, blocks)
    is_last = ra == n_ra - 1
    ready = jnp.maximum(RMAX + 1 - TABLES_LESS * ra, 1)

    def start_loads():
        for_blocks(lambda b: load_sky(b).start())
        load_valid.start()
        load_radii.start()

    @pl.when(jnp.logical_not(is_last))
    def _():
        start_loads()
        for_blocks(pack_only, 0, ahead)

    lax.fori_loop(1, ready, table, 0)
    pl.semaphore_wait(barrier, peers)
    send_rims()

    @pl.when(is_last)
    def _():
        start_loads()
        for_blocks(pack_only, 0, ahead)

    for_blocks(send_packed, 0, ahead)
    lax.fori_loop(ready, RMAX + 1, table, 0)
    spare = xs.shape[0] - rows * CB
    xs[rows * CB:, :] = jnp.zeros((spare, cols), jnp.float32)
    if n_dec == 1:
        hs[...] = jnp.zeros_like(hs)
    load_radii.wait()
    load_valid.wait()
    weights = valid_ref[...].astype(jnp.float32)
    aux[...] = jnp.broadcast_to(jnp.sum(weights, keepdims=True), (8, chans))
    for at, x in enumerate(order):
        vb[at] = jnp.broadcast_to(weights[x:x + 1, :], (CB, cols)).astype(jnp.bfloat16)

    def unpack(low_ref, high_ref, deep, side):
        low = None if side == "high" else low_ref[...].astype(jnp.float32)
        high = None if side == "low" else high_ref[...].astype(jnp.float32)
        for g in range(groups):
            if side != "high":
                left = pltpu.roll(low, (cols - WIDE - WIDE * g) % cols, 2)
            if side != "low":
                right = pltpu.roll(high, (-WIDE * g) % cols, 2)
            on_right = lanes < cols // 2
            if side == "both":
                both = jnp.where(on_right, right, left)
            elif side == "low":
                both = jnp.where(on_right, 0.0, left)
            else:
                both = jnp.where(on_right, right, 0.0)
            hs[g * deep * CB:(g + 1) * deep * CB, :] = both.reshape(deep * CB, cols)

    def unpack_sides(low_ref, high_ref, deep):
        pl.when(has_lo & has_hi)(lambda: unpack(low_ref, high_ref, deep, "both"))
        pl.when(has_lo & jnp.logical_not(has_hi))(lambda: unpack(low_ref, high_ref, deep, "low"))
        pl.when(has_hi & jnp.logical_not(has_lo))(lambda: unpack(low_ref, high_ref, deep, "high"))

    def smooth_columns(b, height, put):
        for c in range(CB):
            rr = radii_ref[b * CB + c]
            main = xs[pl.ds(c, height, stride=CB), :]
            side = hs[pl.ds(c, height, stride=CB), :]
            left_hand = jnp.concatenate([main, side], axis=1).astype(jnp.bfloat16)
            part = jnp.dot(left_hand, tab_dec[rr], preferred_element_type=jnp.float32)
            put(c, part.astype(jnp.bfloat16).astype(jnp.float32))

    def smooth_rows(b, tab, height):
        for c in range(CB):
            rr = radii_ref[b * CB + c]
            column = ps[b, pl.ds(c, ext, stride=CB), :].astype(jnp.bfloat16)
            os[pl.ds(c, height, stride=CB), :] = jnp.dot(
                tab[rr], column, preferred_element_type=jnp.float32
            )

    def gram_of(mine, other, first, height, half=None):
        steps = next(n for n in (8, 6, 4, 2, 1) if height % n == 0)
        if height % 34 == 0:
            steps = 34
        if height % 22 == 0:
            steps = 22

        def gram(i, carry):
            def row(ref, x):
                return ref[:, pl.ds(x, 1), :, :].reshape(chans, cols)

            own = jnp.concatenate([row(mine, i * steps + s) for s in range(steps)], axis=1)
            if half != 0:
                oth = jnp.concatenate([row(other, i * steps + s) for s in range(steps)], axis=1)
            msk = jnp.concatenate([vb[first + i * steps + s] for s in range(steps)], axis=1)
            if half is None:
                across = jnp.concatenate([own, oth], axis=0)
            else:
                across = oth if half else own
            product = lax.dot_general(
                jnp.concatenate([own, msk], axis=0), across,
                (((1,), (1,)), ((), ())), preferred_element_type=jnp.float32,
            )
            if half is None:
                acc[0] += product[:, 0:chans]
                acc[1] += product[:, chans:2 * chans]
            else:
                acc[half] += product
            return carry

        lax.fori_loop(0, height // steps, gram, 0)

    paired = 2 * max((late - SINGLE) // 2, 0)

    def send_edges(b):
        pl.when((b < paired) & (lax.rem(b, 2) == 1))(lambda: ra_both(b - 1, 2, lambda c: c.start()))
        pl.when(b >= paired)(lambda: ra_both(b, 1, lambda c: c.start()))

    def for_edges(b, body):
        pl.when((b < paired) & (lax.rem(b, 2) == 0))(lambda: ra_both(b, 2, body))
        pl.when(b >= paired)(lambda: ra_both(b, 1, body))

    def dec_block(b, carry):
        @pl.when(b + ahead < blocks)
        def _():
            pack_block(b + ahead)

        load_block(b)
        ps[b, rows8 * CB:ext * CB, :] = jnp.zeros(((ext - rows8) * CB, cols), jnp.float32)

        pl.when(has_lo)(lambda: dec_up(b).wait_recv())
        pl.when(has_hi)(lambda: dec_dn(b).wait_recv())
        unpack_sides(halo_lo.at[b], halo_hi.at[b], per)

        def put(c, part):
            ps[b, pl.ds(c, rows8, stride=CB), :] = part

        smooth_columns(b, rows8, put)

        @pl.when(b < late)
        def _():
            edge_lo[b] = ps[b, 0:RMAX * CB, :].reshape(RMAX, CB, cols).astype(jnp.bfloat16)
            last = ps[b, (rows - RMAX) * CB:rows * CB, :]
            edge_hi[b] = last.reshape(RMAX, CB, cols).astype(jnp.bfloat16)
            send_edges(b)

        smooth_rows(b, tab_in, in_rows)
        at = RMAX - in_at
        smooth = os[at * CB:(at + inner) * CB, :].reshape(inner, CB, cols).astype(jnp.bfloat16)
        out_ref[RMAX:rows - RMAX, pl.ds(pl.multiple_of(b * CB, CB), CB), :] = smooth
        mine_in[b] = smooth * vb[2 * RMAX:rows]
        to_twin(1, b).start()
        @pl.when(b == late // 2)
        def _():
            sky_up().wait_recv()
            sky_dn().wait_recv()
            for_blocks(pack_far, 0, blocks - late)

        return carry

    lax.fori_loop(0, blocks, dec_block, 0)

    def far_block(j):
        b = late + j
        here = pl.ds(pl.multiple_of(j * CB, CB), CB)
        for first, ref in ((0, raw_before), (RMAX, raw_after)):
            rim = ref[:, here, :].astype(jnp.float32)
            xs[first * CB:(first + RMAX) * CB, :] = rim.reshape(RMAX * CB, cols)
        pl.when(has_lo)(lambda: far_dec_up(j).wait_recv())
        pl.when(has_hi)(lambda: far_dec_dn(j).wait_recv())
        unpack_sides(far_lo.at[j], far_hi.at[j], far_per)
        height = up(2 * RMAX, 16)

        def put(c, part):
            os[pl.ds(c, height, stride=CB), :] = part

        smooth_columns(b, height, put)
        ps[b, (ext - RMAX) * CB:ext * CB, :] = os[0:RMAX * CB, :]
        ps[b, rows * CB:(rows + RMAX) * CB, :] = os[RMAX * CB:2 * RMAX * CB, :]

    for_blocks(far_block, 0, blocks - late)
    for_blocks(lambda b: to_twin(1, b).wait_recv())
    acc[...] = jnp.zeros_like(acc)
    gram_of(mine_in, other_in, 2 * RMAX, inner)

    def ra_block(i, carry):
        b = lax.rem(i + late, blocks)

        @pl.when(b < late)
        def _():
            for_edges(b, lambda c: c.wait_recv())
            before = z_before[b].astype(jnp.float32)
            ps[b, (ext - RMAX) * CB:ext * CB, :] = before.reshape(RMAX * CB, cols)
            after = z_after[b].astype(jnp.float32)
            ps[b, rows * CB:(rows + RMAX) * CB, :] = after.reshape(RMAX * CB, cols)

        smooth_rows(b, tab_ed, 2 * edge_rows)
        low = os[0:RMAX * CB, :].reshape(RMAX, CB, cols).astype(jnp.bfloat16)
        at = 2 * edge_rows - rows8 + rows - RMAX
        high = os[at * CB:(at + RMAX) * CB, :].reshape(RMAX, CB, cols).astype(jnp.bfloat16)
        here = pl.ds(pl.multiple_of(b * CB, CB), CB)
        out_ref[0:RMAX, here, :] = low
        out_ref[rows - RMAX:rows, here, :] = high
        mine_ed[b, 0:RMAX] = low * vb[0:RMAX]
        mine_ed[b, RMAX:2 * RMAX] = high * vb[RMAX:2 * RMAX]
        to_twin(0, b).start()
        return carry

    lax.fori_loop(0, blocks, ra_block, 0)
    def part_of(p):
        return pl.ds(pl.multiple_of(p * share, share), share)

    def rs(k, p, slot):
        return remote(
            acc.at[k, part_of(p)], shares.at[k, slot], s_rs.at[k, p], r_rs.at[k, slot], peer_id(p)
        )

    def ag(k, p, slot):
        mine = total.at[k, part_of(slot)]
        return remote(mine, mine, s_ag.at[k, p], r_ag.at[k, slot], peer_id(p))

    def au(p, slot):
        return remote(aux, aux_all.at[slot], s_aux.at[p], r_aux.at[slot], peer_id(p))

    def reducing(p, body):
        if reducers == peers:
            body()
        else:
            pl.when(p < reducers)(body)

    gram_of(mine_ed, other_ed, 0, 2 * RMAX, 0)
    each_peer(lambda p: reducing(p, lambda: rs(0, p, rank).start()))
    for_blocks(lambda b: to_twin(0, b).wait_recv())
    gram_of(mine_ed, other_ed, 0, 2 * RMAX, 1)
    each_peer(lambda p: reducing(p, lambda: rs(1, p, rank).start()))
    place = iota((8, chans), 0)
    for k in range(2):
        aux[...] = jnp.where(place == k, acc[k, chans:chans + 8, :], aux[...])
    each_peer(lambda p: au(p, rank).start())
    aux_all[rank] = aux[...]

    def finish(b):
        pl.when(has_hi)(lambda: dec_up(b).wait_send())
        pl.when(has_lo)(lambda: dec_dn(b).wait_send())
        to_twin(0, b).wait_send()
        to_twin(1, b).wait_send()

    def finish_late(b):
        for_edges(b, lambda c: c.wait_send())

    def finish_early(j):
        pl.when(has_hi)(lambda: far_dec_up(j).wait_send())
        pl.when(has_lo)(lambda: far_dec_dn(j).wait_send())

    for_blocks(finish)
    for_blocks(finish_late, 0, late)
    for_blocks(finish_early, 0, blocks - late)
    sky_up().wait_send()
    sky_dn().wait_send()
    def reduce_own(k):
        shares[k, rank] = acc[k, part_of(rank), :]
        each_peer(lambda p: rs(k, rank, p).wait_recv())
        whole = shares[k, 0]
        whole = lax.fori_loop(1, peers, lambda p, t: t + shares[k, p], whole)
        total[k, part_of(rank), :] = whole
        each_peer(lambda p: ag(k, p, rank).start())

    for k in range(2):
        reducing(rank, functools.partial(reduce_own, k))
    each_peer(lambda p: au(p, p).wait_recv())
    sums = lax.fori_loop(1, peers, lambda p, t: t + aux_all[p], aux_all[0])
    count = sums[2:3, 0:1]
    means = sums / count
    mean_ref[...] = means[0:1, :]
    column = jnp.transpose(jnp.broadcast_to(means[0:1, :], (chans, chans)))
    for k in range(2):
        each_peer(lambda p: reducing(p, lambda: ag(k, p, p).wait_recv()))
        block = (total[k] - count * column * means[k:k + 1, :]) / (count - 1.0)
        place = band if k == 0 else 1 - band
        cov_ref[pl.ds(pl.multiple_of(place * chans, chans), chans), :] = jnp.transpose(block)

    for k in range(2):
        each_peer(lambda p: reducing(p, lambda: rs(k, p, rank).wait_send()))
        reducing(rank, lambda: each_peer(lambda p: ag(k, p, rank).wait_send()))
    each_peer(lambda p: au(p, rank).wait_send())


def store(smoothed_ref, mean_ref, cov_ref, smoothed_hbm, mean_hbm, cov_hbm, sems):
    pairs = ((smoothed_ref, smoothed_hbm), (mean_ref, mean_hbm), (cov_ref, cov_hbm))
    copies = [pltpu.make_async_copy(src, dst, sems.at[i]) for i, (src, dst) in enumerate(pairs)]
    for copy in copies:
        copy.start()
    for copy in copies:
        copy.wait()


def per_device(n_ra, n_dec, sky_maps, radii, valid):
    chans, rows, cols = sky_maps.shape
    blocks = chans // CB
    rows8 = up(rows, 16)
    groups = cols // WIDE
    per = -(-rows // groups)
    peers = n_ra * n_dec
    share = chans // min(peers, chans // 8)
    early = early_blocks(blocks)
    far_per = -(-2 * RMAX // groups)
    tall = max(per * groups, rows8)
    f32, b16, dma = jnp.float32, jnp.bfloat16, pltpu.SemaphoreType.DMA
    vmem = pl.BlockSpec(memory_space=pltpu.VMEM)
    hbm = pl.BlockSpec(memory_space=pltpu.HBM)
    in_at, in_rows, edge_rows = inner_rows(rows)
    inner, outer = rows - 2 * RMAX, 2 * RMAX
    flat = pltpu.with_memory_space_constraint(jnp.transpose(sky_maps, (1, 0, 2)), pltpu.HBM)
    radii = pltpu.with_memory_space_constraint(radii, pltpu.HBM)
    valid = pltpu.with_memory_space_constraint(valid, pltpu.HBM)
    packed = pltpu.VMEM((blocks, per, CB, cols), b16)
    far = pltpu.VMEM((early, far_per, CB, cols), b16)
    raw = pltpu.VMEM((RMAX, early * CB, cols), b16)
    edge = pltpu.VMEM((blocks - early, RMAX, CB, cols), b16)
    smoothed, mean, cov = pl.pallas_call(
        functools.partial(kernel, (n_ra, n_dec, rows, chans, cols)),
        out_shape=(
            pltpu.VMEM((rows, chans, cols), b16),
            pltpu.VMEM((1, chans), f32),
            pltpu.VMEM((2 * chans, chans), f32),
        ),
        in_specs=[hbm, hbm, hbm],
        out_specs=(vmem, vmem, vmem),
        scratch_shapes=[
            pltpu.VMEM((rows, chans, cols), b16),
            pltpu.VMEM((rows, cols), jnp.int32),
            pltpu.SMEM((chans,), jnp.int32),
            dma((blocks + 2,)),
            pltpu.VMEM((RMAX + 1, 2 * cols, cols), b16),
            pltpu.VMEM((RMAX + 1, in_rows, 128), b16),
            pltpu.VMEM((RMAX + 1, 2 * edge_rows, 128), b16),
            pltpu.VMEM((tall * CB, cols), f32),
            pltpu.VMEM((tall * CB, cols), f32),
            pltpu.VMEM((rows8 * CB, cols), f32),
            pltpu.VMEM((blocks, 128 * CB, cols), f32),
            pltpu.VMEM((rows, CB, cols), b16),
            pltpu.VMEM((blocks, inner, CB, cols), b16),
            pltpu.VMEM((blocks, outer, CB, cols), b16),
            pltpu.VMEM((blocks, inner, CB, cols), b16),
            pltpu.VMEM((blocks, outer, CB, cols), b16),
            packed, packed, packed, packed,
            far, far, far, far,
            edge, edge, edge, edge, raw, raw,
            pltpu.VMEM((2, chans + CB, chans), f32),
            pltpu.VMEM((2, peers, share, chans), f32),
            pltpu.VMEM((2, chans, chans), f32),
            pltpu.VMEM((8, chans), f32),
            pltpu.VMEM((peers, 8, chans), f32),
            dma((2, blocks + early)), dma((2, blocks + early)),
            dma((2, blocks)), dma((2, blocks)), dma((2, blocks)), dma((2, blocks)),
            dma((2, peers)), dma((2, peers)), dma((2, peers)), dma((2, peers)), dma((peers,)), dma((peers,)),
        ],
        compiler_params=pltpu.CompilerParams(
            collective_id=0, has_side_effects=True, vmem_limit_bytes=40 * 1024 * 1024
        ),
    )(radii, flat, valid)
    smoothed, mean, cov = pl.pallas_call(
        store,
        out_shape=(
            jax.ShapeDtypeStruct((rows, chans, cols), b16),
            jax.ShapeDtypeStruct((1, chans), f32),
            jax.ShapeDtypeStruct((2 * chans, chans), f32),
        ),
        in_specs=(vmem, vmem, vmem),
        out_specs=(hbm, hbm, hbm),
        scratch_shapes=[dma((3,))],
    )(*(pltpu.with_memory_space_constraint(part, pltpu.VMEM) for part in (smoothed, mean, cov)))
    return (jnp.transpose(smoothed, (1, 0, 2)), mean.reshape(chans), cov)


def solution(mesh):
    return jax.shard_map(
        functools.partial(per_device, mesh.shape["ra"], mesh.shape["dec"]),
        mesh=mesh,
        in_specs=(
            P(("groups", "band"), "ra", "dec"),
            P(("groups", "band")),
            P(("groups", "ra"), "dec"),
        ),
        out_specs=(P(("groups", "band"), "ra", "dec"), P(("groups", "band")), P("groups", "band")),
        check_vma=False,
    )
```

```python
import functools

import jax
import jax.numpy as jnp
from jax import lax
from jax.experimental import pallas as pl
from jax.experimental.pallas import tpu as pltpu
from jax.sharding import PartitionSpec as P

RMAX = 17
WIDE = RMAX + 1
CB = 16
EARLY = 2
SINGLE = 2
TABLES_LESS = 6
MESH = pl.DeviceIdType.MESH


def up(value, step):
    return -(-value // step) * step


def iota(shape, dim):
    return lax.broadcasted_iota(jnp.int32, shape, dim)


def early_blocks(blocks):
    return min(EARLY, blocks - 1)


def inner_rows(rows):
    first = RMAX // 16 * 16
    last = up(rows - RMAX, 16)
    return first, last - first, up(RMAX, 8)


def kernel(
    dims, radii_hbm, sky_hbm, valid_hbm, out_ref, mean_ref, cov_ref,
    sky_ref, valid_ref, radii_ref, loads,
    tab_dec, tab_in, tab_ed, xs, hs, os, ps, vb, mine_in, mine_ed, other_in, other_ed,
    pack_up, pack_dn, halo_lo, halo_hi, far_up, far_dn, far_lo, far_hi, edge_lo, edge_hi, z_before, z_after,
    raw_before, raw_after,
    acc, shares, total, ended, column, aux, aux_all,
    s_dec, r_dec, s_ra, r_ra, s_band, r_band, s_rs, r_rs, s_ag, r_ag, s_aux, r_aux,
):
    n_ra, n_dec, rows, chans, cols = dims
    blocks = chans // CB
    rows8 = up(rows, 16)
    groups = cols // WIDE
    per = -(-rows // groups)
    far_per = -(-2 * RMAX // groups)
    late = blocks - early_blocks(blocks)
    peers = n_ra * n_dec
    reducers = min(peers, chans // 16)
    share = chans // reducers
    ext = 128
    in_at, in_rows, edge_rows = inner_rows(rows)
    ra, dec, band = lax.axis_index("ra"), lax.axis_index("dec"), lax.axis_index("band")
    rank = ra * n_dec + dec
    nxt, prv = lax.rem(ra + 1, n_ra), lax.rem(ra + n_ra - 1, n_ra)
    twin = {"band": 1 - band}

    def peer_id(p):
        return {"ra": p // n_dec, "dec": lax.rem(p, n_dec)}

    def each_peer(body):
        if peers <= 8:
            for d in range(1, peers):
                body(lax.rem(rank + d, peers))
            return

        def step(d, carry):
            body(lax.rem(rank + d, peers))
            return carry
        lax.fori_loop(1, peers, step, 0)

    def in_order(body):
        def step(p, carry):
            pl.when(p != rank)(lambda: body(p))
            return carry

        if peers <= 8:
            for p in range(peers):
                step(p, 0)
        else:
            lax.fori_loop(0, peers, step, 0)

    def table(r, carry):
        radius = r.astype(jnp.float32)
        spread = 0.5 * radius
        k = lax.rem(iota((8, cols), 0) - iota((8, cols), 1) + cols + cols // 2, cols) - cols // 2
        k = k.astype(jnp.float32)
        raw = jnp.where(jnp.abs(k) <= radius, jnp.exp(-(k * k) / (2.0 * spread * spread)), 0.0)
        first = raw / jnp.sum(raw, axis=1, keepdims=True)
        full = jnp.concatenate([pltpu.roll(first, 8 * t, 1) for t in range(cols // 8)], axis=0)
        near = jnp.abs(iota((cols, cols), 0) - iota((cols, cols), 1)) <= cols // 2
        tab_in[r] = full[in_at:in_at + in_rows].astype(jnp.bfloat16)
        ends = jnp.concatenate([full[0:edge_rows], full[rows8 - edge_rows:rows8]], axis=0)
        tab_ed[r] = ends.astype(jnp.bfloat16)
        tab_dec[r, 0:cols, :] = jnp.where(near, full, 0.0).astype(jnp.bfloat16)
        tab_dec[r, cols:2 * cols, :] = jnp.where(near, 0.0, full).astype(jnp.bfloat16)
        return carry

    def load_sky(b):
        at = pl.multiple_of(b * CB, CB)
        return pltpu.make_async_copy(
            sky_hbm.at[:, pl.ds(at, CB), :], sky_ref.at[:, pl.ds(at, CB), :], loads.at[b]
        )

    load_valid = pltpu.make_async_copy(valid_hbm, valid_ref, loads.at[blocks])
    load_radii = pltpu.make_async_copy(radii_hbm, radii_ref, loads.at[blocks + 1])
    barrier = pltpu.get_barrier_semaphore()
    each_peer(lambda p: pl.semaphore_signal(barrier, inc=1, device_id=peer_id(p), device_id_type=MESH))
    pl.semaphore_signal(barrier, inc=1, device_id=twin, device_id_type=MESH)

    def for_blocks(body, first=0, last=blocks):
        def step(b, carry):
            body(b)
            return carry
        lax.fori_loop(first, last, step, 0)


    def remote(src, dst, send, recv, target):
        return pltpu.make_async_remote_copy(
            src_ref=src, dst_ref=dst, send_sem=send, recv_sem=recv, device_id=target, device_id_type=MESH
        )

    def dec_up(b):
        return remote(pack_up.at[b], halo_lo.at[b], s_dec.at[0, b], r_dec.at[0, b], {"dec": dec + 1})

    def dec_dn(b):
        return remote(pack_dn.at[b], halo_hi.at[b], s_dec.at[1, b], r_dec.at[1, b], {"dec": dec - 1})

    def far_dec_up(j):
        return remote(
            far_up.at[j], far_lo.at[j], s_dec.at[0, blocks + j], r_dec.at[0, blocks + j], {"dec": dec + 1}
        )

    def far_dec_dn(j):
        return remote(
            far_dn.at[j], far_hi.at[j], s_dec.at[1, blocks + j], r_dec.at[1, blocks + j], {"dec": dec - 1}
        )

    def sky_up():
        rim = sky_hbm.at[pl.ds(rows - RMAX, RMAX), pl.ds(late * CB, chans - late * CB), :]
        return remote(rim, raw_before, s_ra.at[0, late], r_ra.at[0, late], {"ra": nxt})

    def sky_dn():
        rim = sky_hbm.at[pl.ds(0, RMAX), pl.ds(late * CB, chans - late * CB), :]
        return remote(rim, raw_after, s_ra.at[1, late], r_ra.at[1, late], {"ra": prv})

    def ra_up(b, n):
        part = pl.ds(b, n)
        return remote(edge_hi.at[part], z_before.at[part], s_ra.at[0, b], r_ra.at[0, b], {"ra": nxt})

    def ra_dn(b, n):
        part = pl.ds(b, n)
        return remote(edge_lo.at[part], z_after.at[part], s_ra.at[1, b], r_ra.at[1, b], {"ra": prv})

    def ra_both(b, n, body):
        body(ra_up(b, n))
        body(ra_dn(b, n))

    def to_twin(k, b):
        mine, other = ((mine_ed, other_ed), (mine_in, other_in))[k]
        return remote(mine.at[b], other.at[b], s_band.at[k, b], r_band.at[k, b], twin)

    has_hi, has_lo = dec < n_dec - 1, dec > 0
    lanes = iota((1, 1, cols), 2)
    inner = rows - 2 * RMAX
    order = [*range(RMAX), *range(rows - RMAX, rows), *range(RMAX, rows - RMAX)]

    def send_rims():
        @pl.when(ra == 0)
        def _():
            sky_dn().start()
            sky_up().start()

        @pl.when(ra > 0)
        def _():
            sky_up().start()
            sky_dn().start()

    def load_block(b):
        at = pl.multiple_of(b * CB, CB)
        block = sky_ref[:, pl.ds(at, CB), :].astype(jnp.float32)
        xs[0:rows * CB, :] = block.reshape(rows * CB, cols)

    def packed(read, count, deep, first):
        result = jnp.zeros((deep, CB, cols), jnp.float32)
        for g in range(-(-count // deep)):
            end = min(count, (g + 1) * deep)
            part = read(g * deep, end).astype(jnp.float32)
            if end < (g + 1) * deep:
                fill = jnp.zeros(((g + 1) * deep - end, CB, cols), jnp.float32)
                part = jnp.concatenate([part, fill], axis=0)
            turned = pltpu.roll(part, (WIDE * g - first) % cols, 2)
            inside = (lanes >= WIDE * g) & (lanes < WIDE * (g + 1))
            result = jnp.where(inside, turned, result)
        return result.astype(jnp.bfloat16)

    def pack_block(b):
        pack_only(b)
        send_packed(b)

    def send_packed(b):
        pl.when(has_hi)(lambda: dec_up(b).start())
        pl.when(has_lo)(lambda: dec_dn(b).start())

    def pack_only(b):
        load_sky(b).wait()
        at = pl.multiple_of(b * CB, CB)

        def read(first, last):
            return sky_ref[first:last, pl.ds(at, CB), :]

        @pl.when(has_hi)
        def _():
            pack_up[b] = packed(read, rows, per, cols - WIDE)

        @pl.when(has_lo)
        def _():
            pack_dn[b] = packed(read, rows, per, 0)

    def pack_far(j):
        here = pl.ds(pl.multiple_of(j * CB, CB), CB)

        def read(first, last):
            both = []
            if first < RMAX:
                both.append(raw_before[first:min(last, RMAX), here, :])
            if last > RMAX:
                both.append(raw_after[max(first, RMAX) - RMAX:last - RMAX, here, :])
            return jnp.concatenate(both, axis=0)

        @pl.when(has_hi)
        def _():
            far_up[j] = packed(read, 2 * RMAX, far_per, cols - WIDE)
            far_dec_up(j).start()

        @pl.when(has_lo)
        def _():
            far_dn[j] = packed(read, 2 * RMAX, far_per, 0)
            far_dec_dn(j).start()

    ahead = min(2, blocks)
    is_last = ra == n_ra - 1
    ready = jnp.maximum(RMAX + 1 - TABLES_LESS * ra, 1)

    def start_loads():
        for_blocks(lambda b: load_sky(b).start())
        load_valid.start()
        load_radii.start()

    @pl.when(jnp.logical_not(is_last))
    def _():
        start_loads()
        for_blocks(pack_only, 0, ahead)

    lax.fori_loop(1, ready, table, 0)
    pl.semaphore_wait(barrier, peers)
    send_rims()

    @pl.when(is_last)
    def _():
        start_loads()
        for_blocks(pack_only, 0, ahead)

    for_blocks(send_packed, 0, ahead)
    lax.fori_loop(ready, RMAX + 1, table, 0)
    spare = xs.shape[0] - rows * CB
    xs[rows * CB:, :] = jnp.zeros((spare, cols), jnp.float32)
    if n_dec == 1:
        hs[...] = jnp.zeros_like(hs)
    load_radii.wait()
    load_valid.wait()
    weights = valid_ref[...].astype(jnp.float32)
    aux[...] = jnp.broadcast_to(jnp.sum(weights, keepdims=True), (8, chans))
    for at, x in enumerate(order):
        vb[at] = jnp.broadcast_to(weights[x:x + 1, :], (CB, cols)).astype(jnp.bfloat16)

    def unpack(low_ref, high_ref, deep, side):
        low = None if side == "high" else low_ref[...].astype(jnp.float32)
        high = None if side == "low" else high_ref[...].astype(jnp.float32)
        for g in range(groups):
            if side != "high":
                left = pltpu.roll(low, (cols - WIDE - WIDE * g) % cols, 2)
            if side != "low":
                right = pltpu.roll(high, (-WIDE * g) % cols, 2)
            on_right = lanes < cols // 2
            if side == "both":
                both = jnp.where(on_right, right, left)
            elif side == "low":
                both = jnp.where(on_right, 0.0, left)
            else:
                both = jnp.where(on_right, right, 0.0)
            hs[g * deep * CB:(g + 1) * deep * CB, :] = both.reshape(deep * CB, cols)

    def unpack_sides(low_ref, high_ref, deep):
        pl.when(has_lo & has_hi)(lambda: unpack(low_ref, high_ref, deep, "both"))
        pl.when(has_lo & jnp.logical_not(has_hi))(lambda: unpack(low_ref, high_ref, deep, "low"))
        pl.when(has_hi & jnp.logical_not(has_lo))(lambda: unpack(low_ref, high_ref, deep, "high"))

    def smooth_columns(b, height, put):
        for c in range(CB):
            rr = radii_ref[b * CB + c]
            main = xs[pl.ds(c, height, stride=CB), :]
            side = hs[pl.ds(c, height, stride=CB), :]
            left_hand = jnp.concatenate([main, side], axis=1).astype(jnp.bfloat16)
            part = jnp.dot(left_hand, tab_dec[rr], preferred_element_type=jnp.float32)
            put(c, part.astype(jnp.bfloat16).astype(jnp.float32))

    def smooth_rows(b, tab, height):
        for c in range(CB):
            rr = radii_ref[b * CB + c]
            column = ps[b, pl.ds(c, ext, stride=CB), :].astype(jnp.bfloat16)
            os[pl.ds(c, height, stride=CB), :] = jnp.dot(
                tab[rr], column, preferred_element_type=jnp.float32
            )

    def gram_of(mine, other, first, height, half=None):
        steps = next(n for n in (8, 6, 4, 2, 1) if height % n == 0)
        if height % 34 == 0:
            steps = 34
        if height % 22 == 0:
            steps = 22

        def gram(i, carry):
            def row(ref, x):
                return ref[:, pl.ds(x, 1), :, :].reshape(chans, cols)

            own = jnp.concatenate([row(mine, i * steps + s) for s in range(steps)], axis=1)
            if half != 0:
                oth = jnp.concatenate([row(other, i * steps + s) for s in range(steps)], axis=1)
            msk = jnp.concatenate([vb[first + i * steps + s] for s in range(steps)], axis=1)
            if half is None:
                across = jnp.concatenate([own, oth], axis=0)
            else:
                across = oth if half else own
            product = lax.dot_general(
                jnp.concatenate([own, msk], axis=0), across,
                (((1,), (1,)), ((), ())), preferred_element_type=jnp.float32,
            )
            if half is None:
                acc[0] += product[:, 0:chans]
                acc[1] += product[:, chans:2 * chans]
            else:
                acc[half] += product
            return carry

        lax.fori_loop(0, height // steps, gram, 0)

    paired = 2 * max((late - SINGLE) // 2, 0)

    def send_edges(b):
        pl.when((b < paired) & (lax.rem(b, 2) == 1))(lambda: ra_both(b - 1, 2, lambda c: c.start()))
        pl.when(b >= paired)(lambda: ra_both(b, 1, lambda c: c.start()))

    def for_edges(b, body):
        pl.when((b < paired) & (lax.rem(b, 2) == 0))(lambda: ra_both(b, 2, body))
        pl.when(b >= paired)(lambda: ra_both(b, 1, body))

    def dec_block(b, carry):
        @pl.when(b + ahead < blocks)
        def _():
            pack_block(b + ahead)

        load_block(b)
        ps[b, rows8 * CB:ext * CB, :] = jnp.zeros(((ext - rows8) * CB, cols), jnp.float32)

        pl.when(has_lo)(lambda: dec_up(b).wait_recv())
        pl.when(has_hi)(lambda: dec_dn(b).wait_recv())
        unpack_sides(halo_lo.at[b], halo_hi.at[b], per)

        def put(c, part):
            ps[b, pl.ds(c, rows8, stride=CB), :] = part

        smooth_columns(b, rows8, put)

        @pl.when(b < late)
        def _():
            edge_lo[b] = ps[b, 0:RMAX * CB, :].reshape(RMAX, CB, cols).astype(jnp.bfloat16)
            last = ps[b, (rows - RMAX) * CB:rows * CB, :]
            edge_hi[b] = last.reshape(RMAX, CB, cols).astype(jnp.bfloat16)
            send_edges(b)

        smooth_rows(b, tab_in, in_rows)
        at = RMAX - in_at
        smooth = os[at * CB:(at + inner) * CB, :].reshape(inner, CB, cols).astype(jnp.bfloat16)
        out_ref[RMAX:rows - RMAX, pl.ds(pl.multiple_of(b * CB, CB), CB), :] = smooth
        mine_in[b] = smooth * vb[2 * RMAX:rows]
        to_twin(1, b).start()
        @pl.when(b == late // 2)
        def _():
            sky_up().wait_recv()
            sky_dn().wait_recv()
            for_blocks(pack_far, 0, blocks - late)

        return carry

    lax.fori_loop(0, blocks, dec_block, 0)

    def far_block(j):
        b = late + j
        here = pl.ds(pl.multiple_of(j * CB, CB), CB)
        for first, ref in ((0, raw_before), (RMAX, raw_after)):
            rim = ref[:, here, :].astype(jnp.float32)
            xs[first * CB:(first + RMAX) * CB, :] = rim.reshape(RMAX * CB, cols)
        pl.when(has_lo)(lambda: far_dec_up(j).wait_recv())
        pl.when(has_hi)(lambda: far_dec_dn(j).wait_recv())
        unpack_sides(far_lo.at[j], far_hi.at[j], far_per)
        height = up(2 * RMAX, 16)

        def put(c, part):
            os[pl.ds(c, height, stride=CB), :] = part

        smooth_columns(b, height, put)
        ps[b, (ext - RMAX) * CB:ext * CB, :] = os[0:RMAX * CB, :]
        ps[b, rows * CB:(rows + RMAX) * CB, :] = os[RMAX * CB:2 * RMAX * CB, :]

    for_blocks(far_block, 0, blocks - late)
    for_blocks(lambda b: to_twin(1, b).wait_recv())
    acc[...] = jnp.zeros_like(acc)
    gram_of(mine_in, other_in, 2 * RMAX, inner)

    def ra_block(i, carry):
        b = lax.rem(i + late, blocks)

        @pl.when(b < late)
        def _():
            for_edges(b, lambda c: c.wait_recv())
            before = z_before[b].astype(jnp.float32)
            ps[b, (ext - RMAX) * CB:ext * CB, :] = before.reshape(RMAX * CB, cols)
            after = z_after[b].astype(jnp.float32)
            ps[b, rows * CB:(rows + RMAX) * CB, :] = after.reshape(RMAX * CB, cols)

        smooth_rows(b, tab_ed, 2 * edge_rows)
        low = os[0:RMAX * CB, :].reshape(RMAX, CB, cols).astype(jnp.bfloat16)
        at = 2 * edge_rows - rows8 + rows - RMAX
        high = os[at * CB:(at + RMAX) * CB, :].reshape(RMAX, CB, cols).astype(jnp.bfloat16)
        here = pl.ds(pl.multiple_of(b * CB, CB), CB)
        out_ref[0:RMAX, here, :] = low
        out_ref[rows - RMAX:rows, here, :] = high
        mine_ed[b, 0:RMAX] = low * vb[0:RMAX]
        mine_ed[b, RMAX:2 * RMAX] = high * vb[RMAX:2 * RMAX]
        to_twin(0, b).start()
        return carry

    lax.fori_loop(0, blocks, ra_block, 0)
    def part_of(p):
        return pl.ds(pl.multiple_of(p * share, share), share)

    def rs(k, p, slot):
        return remote(
            acc.at[k, part_of(p)], shares.at[k, slot], s_rs.at[k, p], r_rs.at[k, slot], peer_id(p)
        )

    def ag(k, p, slot):
        mine = (total, ended)[k].at[part_of(slot)]
        return remote(mine, mine, s_ag.at[k, p], r_ag.at[k, slot], peer_id(p))

    def au(p, slot):
        return remote(aux, aux_all.at[slot], s_aux.at[p], r_aux.at[slot], peer_id(p))

    def reducing(p, body):
        if reducers == peers:
            body()
        else:
            pl.when(p < reducers)(body)

    gram_of(mine_ed, other_ed, 0, 2 * RMAX, 0)
    each_peer(lambda p: reducing(p, lambda: rs(0, p, rank).start()))
    for_blocks(lambda b: to_twin(0, b).wait_recv())
    gram_of(mine_ed, other_ed, 0, 2 * RMAX, 1)
    place = iota((8, chans), 0)
    for k in range(2):
        aux[...] = jnp.where(place == k, acc[k, chans:chans + 8, :], aux[...])
    each_peer(lambda p: au(p, rank).start())
    each_peer(lambda p: reducing(p, lambda: rs(1, p, rank).start()))
    aux_all[rank] = aux[...]

    def finish(b):
        pl.when(has_hi)(lambda: dec_up(b).wait_send())
        pl.when(has_lo)(lambda: dec_dn(b).wait_send())
        to_twin(0, b).wait_send()
        to_twin(1, b).wait_send()

    def finish_late(b):
        for_edges(b, lambda c: c.wait_send())

    def finish_early(j):
        pl.when(has_hi)(lambda: far_dec_up(j).wait_send())
        pl.when(has_lo)(lambda: far_dec_dn(j).wait_send())

    for_blocks(finish)
    for_blocks(finish_late, 0, late)
    for_blocks(finish_early, 0, blocks - late)
    sky_up().wait_send()
    sky_dn().wait_send()
    def whole_of(k):
        shares[k, rank] = acc[k, part_of(rank), :]
        each_peer(lambda p: rs(k, rank, p).wait_recv())
        return lax.fori_loop(1, peers, lambda p, t: t + shares[k, p], shares[k, 0])

    def reduce_first():
        total[part_of(rank), :] = whole_of(0)
        in_order(lambda p: ag(0, p, rank).start())

    reducing(rank, reduce_first)
    each_peer(lambda p: au(p, p).wait_recv())
    sums = lax.fori_loop(1, peers, lambda p, t: t + aux_all[p], aux_all[0])
    count = sums[2:3, 0:1]
    means = sums / count
    mean_ref[...] = means[0:1, :]
    column[...] = jnp.transpose(jnp.broadcast_to(means[0:1, :], (chans, chans)))

    def reduce_second():
        block = whole_of(1) - count * column[part_of(rank), :] * means[1:2, :]
        ended[part_of(rank), :] = (block / (count - 1.0)).astype(jnp.bfloat16)
        in_order(lambda p: ag(1, p, rank).start())

    reducing(rank, reduce_second)
    each_peer(lambda p: au(p, rank).wait_send())
    for k in range(2):
        each_peer(lambda p: reducing(p, lambda: rs(k, p, rank).wait_send()))
    for k in range(2):
        each_peer(lambda p: reducing(p, lambda: ag(k, p, p).wait_recv()))
        place = band if k == 0 else 1 - band
        if k == 0:
            block = (total[...] - count * column[...] * means[0:1, :]) / (count - 1.0)
        else:
            block = ended[...].astype(jnp.float32)
        cov_ref[pl.ds(pl.multiple_of(place * chans, chans), chans), :] = jnp.transpose(block)
    for k in range(2):
        reducing(rank, lambda: each_peer(lambda p: ag(k, p, rank).wait_send()))


def store(smoothed_ref, mean_ref, cov_ref, smoothed_hbm, mean_hbm, cov_hbm, sems):
    pairs = ((smoothed_ref, smoothed_hbm), (mean_ref, mean_hbm), (cov_ref, cov_hbm))
    copies = [pltpu.make_async_copy(src, dst, sems.at[i]) for i, (src, dst) in enumerate(pairs)]
    for copy in copies:
        copy.start()
    for copy in copies:
        copy.wait()


def per_device(n_ra, n_dec, sky_maps, radii, valid):
    chans, rows, cols = sky_maps.shape
    blocks = chans // CB
    rows8 = up(rows, 16)
    groups = cols // WIDE
    per = -(-rows // groups)
    peers = n_ra * n_dec
    share = chans // min(peers, chans // 16)
    early = early_blocks(blocks)
    far_per = -(-2 * RMAX // groups)
    tall = max(per * groups, rows8)
    f32, b16, dma = jnp.float32, jnp.bfloat16, pltpu.SemaphoreType.DMA
    vmem = pl.BlockSpec(memory_space=pltpu.VMEM)
    hbm = pl.BlockSpec(memory_space=pltpu.HBM)
    in_at, in_rows, edge_rows = inner_rows(rows)
    inner, outer = rows - 2 * RMAX, 2 * RMAX
    flat = pltpu.with_memory_space_constraint(jnp.transpose(sky_maps, (1, 0, 2)), pltpu.HBM)
    radii = pltpu.with_memory_space_constraint(radii, pltpu.HBM)
    valid = pltpu.with_memory_space_constraint(valid, pltpu.HBM)
    packed = pltpu.VMEM((blocks, per, CB, cols), b16)
    far = pltpu.VMEM((early, far_per, CB, cols), b16)
    raw = pltpu.VMEM((RMAX, early * CB, cols), b16)
    edge = pltpu.VMEM((blocks - early, RMAX, CB, cols), b16)
    smoothed, mean, cov = pl.pallas_call(
        functools.partial(kernel, (n_ra, n_dec, rows, chans, cols)),
        out_shape=(
            pltpu.VMEM((rows, chans, cols), b16),
            pltpu.VMEM((1, chans), f32),
            pltpu.VMEM((2 * chans, chans), f32),
        ),
        in_specs=[hbm, hbm, hbm],
        out_specs=(vmem, vmem, vmem),
        scratch_shapes=[
            pltpu.VMEM((rows, chans, cols), b16),
            pltpu.VMEM((rows, cols), jnp.int32),
            pltpu.SMEM((chans,), jnp.int32),
            dma((blocks + 2,)),
            pltpu.VMEM((RMAX + 1, 2 * cols, cols), b16),
            pltpu.VMEM((RMAX + 1, in_rows, 128), b16),
            pltpu.VMEM((RMAX + 1, 2 * edge_rows, 128), b16),
            pltpu.VMEM((tall * CB, cols), f32),
            pltpu.VMEM((tall * CB, cols), f32),
            pltpu.VMEM((rows8 * CB, cols), f32),
            pltpu.VMEM((blocks, 128 * CB, cols), f32),
            pltpu.VMEM((rows, CB, cols), b16),
            pltpu.VMEM((blocks, inner, CB, cols), b16),
            pltpu.VMEM((blocks, outer, CB, cols), b16),
            pltpu.VMEM((blocks, inner, CB, cols), b16),
            pltpu.VMEM((blocks, outer, CB, cols), b16),
            packed, packed, packed, packed,
            far, far, far, far,
            edge, edge, edge, edge, raw, raw,
            pltpu.VMEM((2, chans + CB, chans), f32),
            pltpu.VMEM((2, peers, share, chans), f32),
            pltpu.VMEM((chans, chans), f32),
            pltpu.VMEM((chans, chans), b16),
            pltpu.VMEM((chans, chans), f32),
            pltpu.VMEM((8, chans), f32),
            pltpu.VMEM((peers, 8, chans), f32),
            dma((2, blocks + early)), dma((2, blocks + early)),
            dma((2, blocks)), dma((2, blocks)), dma((2, blocks)), dma((2, blocks)),
            dma((2, peers)), dma((2, peers)), dma((2, peers)), dma((2, peers)), dma((peers,)), dma((peers,)),
        ],
        compiler_params=pltpu.CompilerParams(
            collective_id=0, has_side_effects=True, vmem_limit_bytes=40 * 1024 * 1024
        ),
    )(radii, flat, valid)
    smoothed, mean, cov = pl.pallas_call(
        store,
        out_shape=(
            jax.ShapeDtypeStruct((rows, chans, cols), b16),
            jax.ShapeDtypeStruct((1, chans), f32),
            jax.ShapeDtypeStruct((2 * chans, chans), f32),
        ),
        in_specs=(vmem, vmem, vmem),
        out_specs=(hbm, hbm, hbm),
        scratch_shapes=[dma((3,))],
    )(*(pltpu.with_memory_space_constraint(part, pltpu.VMEM) for part in (smoothed, mean, cov)))
    return (jnp.transpose(smoothed, (1, 0, 2)), mean.reshape(chans), cov)


def solution(mesh):
    return jax.shard_map(
        functools.partial(per_device, mesh.shape["ra"], mesh.shape["dec"]),
        mesh=mesh,
        in_specs=(
            P(("groups", "band"), "ra", "dec"),
            P(("groups", "band")),
            P(("groups", "ra"), "dec"),
        ),
        out_specs=(P(("groups", "band"), "ra", "dec"), P(("groups", "band")), P("groups", "band")),
        check_vma=False,
    )
```

```python
import functools

import jax
import jax.numpy as jnp
from jax import lax
from jax.experimental import pallas as pl
from jax.experimental.pallas import tpu as pltpu
from jax.sharding import PartitionSpec as P

RMAX = 17
WIDE = RMAX + 1
CB = 16
EARLY = 2
SINGLE = 2
TABLES_LESS = 6
MESH = pl.DeviceIdType.MESH


def up(value, step):
    return -(-value // step) * step


def iota(shape, dim):
    return lax.broadcasted_iota(jnp.int32, shape, dim)


def early_blocks(blocks):
    return min(EARLY, blocks - 1)


def inner_rows(rows):
    first = RMAX // 16 * 16
    last = up(rows - RMAX, 16)
    return first, last - first, up(RMAX, 8)


def kernel(
    dims, radii_hbm, sky_hbm, valid_hbm, out_ref, mean_ref, cov_ref,
    sky_ref, valid_ref, radii_ref, loads,
    tab_dec, tab_in, tab_ed, xs, hs, os, ps, vb, mine_in, mine_ed, other_in, other_ed,
    pack_up, pack_dn, halo_lo, halo_hi, far_up, far_dn, far_lo, far_hi, edge_lo, edge_hi, z_before, z_after,
    raw_before, raw_after,
    acc, shares, total, aux, aux_all,
    s_dec, r_dec, s_ra, r_ra, s_band, r_band, s_rs, r_rs, s_ag, r_ag, s_aux, r_aux,
):
    n_ra, n_dec, rows, chans, cols = dims
    blocks = chans // CB
    rows8 = up(rows, 16)
    groups = cols // WIDE
    per = -(-rows // groups)
    far_per = -(-2 * RMAX // groups)
    late = blocks - early_blocks(blocks)
    peers = n_ra * n_dec
    reducers = min(peers, chans // 8)
    share = chans // reducers
    ext = 128
    in_at, in_rows, edge_rows = inner_rows(rows)
    ra, dec, band = lax.axis_index("ra"), lax.axis_index("dec"), lax.axis_index("band")
    rank = ra * n_dec + dec
    nxt, prv = lax.rem(ra + 1, n_ra), lax.rem(ra + n_ra - 1, n_ra)
    twin = {"band": 1 - band}

    def peer_id(p):
        return {"ra": p // n_dec, "dec": lax.rem(p, n_dec)}

    def each_peer(body):
        if peers <= 8:
            for d in range(1, peers):
                body(lax.rem(rank + d, peers))
            return

        def step(d, carry):
            body(lax.rem(rank + d, peers))
            return carry
        lax.fori_loop(1, peers, step, 0)

    def in_order(body):
        def step(p, carry):
            pl.when(p != rank)(lambda: body(p))
            return carry

        if peers <= 8:
            for p in range(peers):
                step(p, 0)
        else:
            lax.fori_loop(0, peers, step, 0)

    def table(r, carry):
        radius = r.astype(jnp.float32)
        spread = 0.5 * radius
        k = lax.rem(iota((8, cols), 0) - iota((8, cols), 1) + cols + cols // 2, cols) - cols // 2
        k = k.astype(jnp.float32)
        raw = jnp.where(jnp.abs(k) <= radius, jnp.exp(-(k * k) / (2.0 * spread * spread)), 0.0)
        first = raw / jnp.sum(raw, axis=1, keepdims=True)
        full = jnp.concatenate([pltpu.roll(first, 8 * t, 1) for t in range(cols // 8)], axis=0)
        near = jnp.abs(iota((cols, cols), 0) - iota((cols, cols), 1)) <= cols // 2
        tab_in[r] = full[in_at:in_at + in_rows].astype(jnp.bfloat16)
        ends = jnp.concatenate([full[0:edge_rows], full[rows8 - edge_rows:rows8]], axis=0)
        tab_ed[r] = ends.astype(jnp.bfloat16)
        tab_dec[r, 0:cols, :] = jnp.where(near, full, 0.0).astype(jnp.bfloat16)
        tab_dec[r, cols:2 * cols, :] = jnp.where(near, 0.0, full).astype(jnp.bfloat16)
        return carry

    def load_sky(b):
        at = pl.multiple_of(b * CB, CB)
        return pltpu.make_async_copy(
            sky_hbm.at[:, pl.ds(at, CB), :], sky_ref.at[:, pl.ds(at, CB), :], loads.at[b]
        )

    load_valid = pltpu.make_async_copy(valid_hbm, valid_ref, loads.at[blocks])
    load_radii = pltpu.make_async_copy(radii_hbm, radii_ref, loads.at[blocks + 1])
    barrier = pltpu.get_barrier_semaphore()
    each_peer(lambda p: pl.semaphore_signal(barrier, inc=1, device_id=peer_id(p), device_id_type=MESH))
    pl.semaphore_signal(barrier, inc=1, device_id=twin, device_id_type=MESH)

    def for_blocks(body, first=0, last=blocks):
        def step(b, carry):
            body(b)
            return carry
        lax.fori_loop(first, last, step, 0)


    def remote(src, dst, send, recv, target):
        return pltpu.make_async_remote_copy(
            src_ref=src, dst_ref=dst, send_sem=send, recv_sem=recv, device_id=target, device_id_type=MESH
        )

    def dec_up(b):
        return remote(pack_up.at[b], halo_lo.at[b], s_dec.at[0, b], r_dec.at[0, b], {"dec": dec + 1})

    def dec_dn(b):
        return remote(pack_dn.at[b], halo_hi.at[b], s_dec.at[1, b], r_dec.at[1, b], {"dec": dec - 1})

    def far_dec_up(j):
        return remote(
            far_up.at[j], far_lo.at[j], s_dec.at[0, blocks + j], r_dec.at[0, blocks + j], {"dec": dec + 1}
        )

    def far_dec_dn(j):
        return remote(
            far_dn.at[j], far_hi.at[j], s_dec.at[1, blocks + j], r_dec.at[1, blocks + j], {"dec": dec - 1}
        )

    def sky_up():
        rim = sky_hbm.at[pl.ds(rows - RMAX, RMAX), pl.ds(late * CB, chans - late * CB), :]
        return remote(rim, raw_before, s_ra.at[0, late], r_ra.at[0, late], {"ra": nxt})

    def sky_dn():
        rim = sky_hbm.at[pl.ds(0, RMAX), pl.ds(late * CB, chans - late * CB), :]
        return remote(rim, raw_after, s_ra.at[1, late], r_ra.at[1, late], {"ra": prv})

    def ra_up(b, n):
        part = pl.ds(b, n)
        return remote(edge_hi.at[part], z_before.at[part], s_ra.at[0, b], r_ra.at[0, b], {"ra": nxt})

    def ra_dn(b, n):
        part = pl.ds(b, n)
        return remote(edge_lo.at[part], z_after.at[part], s_ra.at[1, b], r_ra.at[1, b], {"ra": prv})

    def ra_both(b, n, body):
        body(ra_up(b, n))
        body(ra_dn(b, n))

    def to_twin(k, b):
        mine, other = ((mine_ed, other_ed), (mine_in, other_in))[k]
        return remote(mine.at[b], other.at[b], s_band.at[k, b], r_band.at[k, b], twin)

    has_hi, has_lo = dec < n_dec - 1, dec > 0
    lanes = iota((1, 1, cols), 2)
    inner = rows - 2 * RMAX
    order = [*range(RMAX), *range(rows - RMAX, rows), *range(RMAX, rows - RMAX)]

    def send_rims():
        @pl.when(ra == 0)
        def _():
            sky_dn().start()
            sky_up().start()

        @pl.when(ra > 0)
        def _():
            sky_up().start()
            sky_dn().start()

    def load_block(b):
        at = pl.multiple_of(b * CB, CB)
        block = sky_ref[:, pl.ds(at, CB), :].astype(jnp.float32)
        xs[0:rows * CB, :] = block.reshape(rows * CB, cols)

    def packed(read, count, deep, first):
        result = jnp.zeros((deep, CB, cols), jnp.float32)
        for g in range(-(-count // deep)):
            end = min(count, (g + 1) * deep)
            part = read(g * deep, end).astype(jnp.float32)
            if end < (g + 1) * deep:
                fill = jnp.zeros(((g + 1) * deep - end, CB, cols), jnp.float32)
                part = jnp.concatenate([part, fill], axis=0)
            turned = pltpu.roll(part, (WIDE * g - first) % cols, 2)
            inside = (lanes >= WIDE * g) & (lanes < WIDE * (g + 1))
            result = jnp.where(inside, turned, result)
        return result.astype(jnp.bfloat16)

    def pack_block(b):
        pack_only(b)
        send_packed(b)

    def send_packed(b):
        pl.when(has_hi)(lambda: dec_up(b).start())
        pl.when(has_lo)(lambda: dec_dn(b).start())

    def pack_only(b):
        load_sky(b).wait()
        at = pl.multiple_of(b * CB, CB)

        def read(first, last):
            return sky_ref[first:last, pl.ds(at, CB), :]

        @pl.when(has_hi)
        def _():
            pack_up[b] = packed(read, rows, per, cols - WIDE)

        @pl.when(has_lo)
        def _():
            pack_dn[b] = packed(read, rows, per, 0)

    def pack_far(j):
        here = pl.ds(pl.multiple_of(j * CB, CB), CB)

        def read(first, last):
            both = []
            if first < RMAX:
                both.append(raw_before[first:min(last, RMAX), here, :])
            if last > RMAX:
                both.append(raw_after[max(first, RMAX) - RMAX:last - RMAX, here, :])
            return jnp.concatenate(both, axis=0)

        @pl.when(has_hi)
        def _():
            far_up[j] = packed(read, 2 * RMAX, far_per, cols - WIDE)
            far_dec_up(j).start()

        @pl.when(has_lo)
        def _():
            far_dn[j] = packed(read, 2 * RMAX, far_per, 0)
            far_dec_dn(j).start()

    ahead = min(2, blocks)
    is_last = ra == n_ra - 1
    ready = jnp.maximum(RMAX + 1 - TABLES_LESS * ra, 1)

    def start_loads():
        for_blocks(lambda b: load_sky(b).start())
        load_valid.start()
        load_radii.start()

    @pl.when(jnp.logical_not(is_last))
    def _():
        start_loads()
        for_blocks(pack_only, 0, ahead)

    lax.fori_loop(1, ready, table, 0)
    pl.semaphore_wait(barrier, peers)
    send_rims()

    @pl.when(is_last)
    def _():
        start_loads()
        for_blocks(pack_only, 0, ahead)

    for_blocks(send_packed, 0, ahead)
    lax.fori_loop(ready, RMAX + 1, table, 0)
    spare = xs.shape[0] - rows * CB
    xs[rows * CB:, :] = jnp.zeros((spare, cols), jnp.float32)
    if n_dec == 1:
        hs[...] = jnp.zeros_like(hs)
    load_radii.wait()
    load_valid.wait()
    weights = valid_ref[...].astype(jnp.float32)
    aux[...] = jnp.broadcast_to(jnp.sum(weights, keepdims=True), (8, chans))
    for at, x in enumerate(order):
        vb[at] = jnp.broadcast_to(weights[x:x + 1, :], (CB, cols)).astype(jnp.bfloat16)

    def unpack(low_ref, high_ref, deep, side):
        low = None if side == "high" else low_ref[...].astype(jnp.float32)
        high = None if side == "low" else high_ref[...].astype(jnp.float32)
        for g in range(groups):
            if side != "high":
                left = pltpu.roll(low, (cols - WIDE - WIDE * g) % cols, 2)
            if side != "low":
                right = pltpu.roll(high, (-WIDE * g) % cols, 2)
            on_right = lanes < cols // 2
            if side == "both":
                both = jnp.where(on_right, right, left)
            elif side == "low":
                both = jnp.where(on_right, 0.0, left)
            else:
                both = jnp.where(on_right, right, 0.0)
            hs[g * deep * CB:(g + 1) * deep * CB, :] = both.reshape(deep * CB, cols)

    def unpack_sides(low_ref, high_ref, deep):
        pl.when(has_lo & has_hi)(lambda: unpack(low_ref, high_ref, deep, "both"))
        pl.when(has_lo & jnp.logical_not(has_hi))(lambda: unpack(low_ref, high_ref, deep, "low"))
        pl.when(has_hi & jnp.logical_not(has_lo))(lambda: unpack(low_ref, high_ref, deep, "high"))

    def smooth_columns(b, height, put):
        for c in range(CB):
            rr = radii_ref[b * CB + c]
            main = xs[pl.ds(c, height, stride=CB), :]
            side = hs[pl.ds(c, height, stride=CB), :]
            left_hand = jnp.concatenate([main, side], axis=1).astype(jnp.bfloat16)
            part = jnp.dot(left_hand, tab_dec[rr], preferred_element_type=jnp.float32)
            put(c, part.astype(jnp.bfloat16).astype(jnp.float32))

    def smooth_rows(b, tab, height):
        for c in range(CB):
            rr = radii_ref[b * CB + c]
            column = ps[b, pl.ds(c, ext, stride=CB), :].astype(jnp.bfloat16)
            os[pl.ds(c, height, stride=CB), :] = jnp.dot(
                tab[rr], column, preferred_element_type=jnp.float32
            )

    def gram_of(mine, other, first, height, half=None):
        steps = next(n for n in (8, 6, 4, 2, 1) if height % n == 0)
        if height % 34 == 0:
            steps = 34
        if height % 22 == 0:
            steps = 22

        def gram(i, carry):
            def row(ref, x):
                return ref[:, pl.ds(x, 1), :, :].reshape(chans, cols)

            own = jnp.concatenate([row(mine, i * steps + s) for s in range(steps)], axis=1)
            if half != 0:
                oth = jnp.concatenate([row(other, i * steps + s) for s in range(steps)], axis=1)
            msk = jnp.concatenate([vb[first + i * steps + s] for s in range(steps)], axis=1)
            if half is None:
                across = jnp.concatenate([own, oth], axis=0)
            else:
                across = oth if half else own
            product = lax.dot_general(
                jnp.concatenate([own, msk], axis=0), across,
                (((1,), (1,)), ((), ())), preferred_element_type=jnp.float32,
            )
            if half is None:
                acc[0] += product[:, 0:chans]
                acc[1] += product[:, chans:2 * chans]
            else:
                acc[half] += product
            return carry

        lax.fori_loop(0, height // steps, gram, 0)

    paired = 2 * max((late - SINGLE) // 2, 0)

    def send_edges(b):
        pl.when((b < paired) & (lax.rem(b, 2) == 1))(lambda: ra_both(b - 1, 2, lambda c: c.start()))
        pl.when(b >= paired)(lambda: ra_both(b, 1, lambda c: c.start()))

    def for_edges(b, body):
        pl.when((b < paired) & (lax.rem(b, 2) == 0))(lambda: ra_both(b, 2, body))
        pl.when(b >= paired)(lambda: ra_both(b, 1, body))

    def dec_block(b, carry):
        @pl.when(b + ahead < blocks)
        def _():
            pack_block(b + ahead)

        load_block(b)
        ps[b, rows8 * CB:ext * CB, :] = jnp.zeros(((ext - rows8) * CB, cols), jnp.float32)

        pl.when(has_lo)(lambda: dec_up(b).wait_recv())
        pl.when(has_hi)(lambda: dec_dn(b).wait_recv())
        unpack_sides(halo_lo.at[b], halo_hi.at[b], per)

        def put(c, part):
            ps[b, pl.ds(c, rows8, stride=CB), :] = part

        smooth_columns(b, rows8, put)

        @pl.when(b < late)
        def _():
            edge_lo[b] = ps[b, 0:RMAX * CB, :].reshape(RMAX, CB, cols).astype(jnp.bfloat16)
            last = ps[b, (rows - RMAX) * CB:rows * CB, :]
            edge_hi[b] = last.reshape(RMAX, CB, cols).astype(jnp.bfloat16)
            send_edges(b)

        smooth_rows(b, tab_in, in_rows)
        at = RMAX - in_at
        smooth = os[at * CB:(at + inner) * CB, :].reshape(inner, CB, cols).astype(jnp.bfloat16)
        out_ref[RMAX:rows - RMAX, pl.ds(pl.multiple_of(b * CB, CB), CB), :] = smooth
        mine_in[b] = smooth * vb[2 * RMAX:rows]
        to_twin(1, b).start()
        @pl.when(b == late // 2)
        def _():
            sky_up().wait_recv()
            sky_dn().wait_recv()
            for_blocks(pack_far, 0, blocks - late)

        return carry

    lax.fori_loop(0, blocks, dec_block, 0)

    def far_block(j):
        b = late + j
        here = pl.ds(pl.multiple_of(j * CB, CB), CB)
        for first, ref in ((0, raw_before), (RMAX, raw_after)):
            rim = ref[:, here, :].astype(jnp.float32)
            xs[first * CB:(first + RMAX) * CB, :] = rim.reshape(RMAX * CB, cols)
        pl.when(has_lo)(lambda: far_dec_up(j).wait_recv())
        pl.when(has_hi)(lambda: far_dec_dn(j).wait_recv())
        unpack_sides(far_lo.at[j], far_hi.at[j], far_per)
        height = up(2 * RMAX, 16)

        def put(c, part):
            os[pl.ds(c, height, stride=CB), :] = part

        smooth_columns(b, height, put)
        ps[b, (ext - RMAX) * CB:ext * CB, :] = os[0:RMAX * CB, :]
        ps[b, rows * CB:(rows + RMAX) * CB, :] = os[RMAX * CB:2 * RMAX * CB, :]

    for_blocks(far_block, 0, blocks - late)
    for_blocks(lambda b: to_twin(1, b).wait_recv())
    acc[...] = jnp.zeros_like(acc)
    gram_of(mine_in, other_in, 2 * RMAX, inner)

    def ra_block(i, carry):
        b = lax.rem(i + late, blocks)

        @pl.when(b < late)
        def _():
            for_edges(b, lambda c: c.wait_recv())
            before = z_before[b].astype(jnp.float32)
            ps[b, (ext - RMAX) * CB:ext * CB, :] = before.reshape(RMAX * CB, cols)
            after = z_after[b].astype(jnp.float32)
            ps[b, rows * CB:(rows + RMAX) * CB, :] = after.reshape(RMAX * CB, cols)

        smooth_rows(b, tab_ed, 2 * edge_rows)
        low = os[0:RMAX * CB, :].reshape(RMAX, CB, cols).astype(jnp.bfloat16)
        at = 2 * edge_rows - rows8 + rows - RMAX
        high = os[at * CB:(at + RMAX) * CB, :].reshape(RMAX, CB, cols).astype(jnp.bfloat16)
        here = pl.ds(pl.multiple_of(b * CB, CB), CB)
        out_ref[0:RMAX, here, :] = low
        out_ref[rows - RMAX:rows, here, :] = high
        mine_ed[b, 0:RMAX] = low * vb[0:RMAX]
        mine_ed[b, RMAX:2 * RMAX] = high * vb[RMAX:2 * RMAX]
        to_twin(0, b).start()
        return carry

    lax.fori_loop(0, blocks, ra_block, 0)
    def part_of(p):
        return pl.ds(pl.multiple_of(p * share, share), share)

    def rs(k, p, slot):
        return remote(
            acc.at[k, part_of(p)], shares.at[k, slot], s_rs.at[k, p], r_rs.at[k, slot], peer_id(p)
        )

    def ag(k, p, slot):
        mine = total.at[k, part_of(slot)]
        return remote(mine, mine, s_ag.at[k, p], r_ag.at[k, slot], peer_id(p))

    def au(p, slot):
        return remote(aux, aux_all.at[slot], s_aux.at[p], r_aux.at[slot], peer_id(p))

    def reducing(p, body):
        if reducers == peers:
            body()
        else:
            pl.when(p < reducers)(body)

    gram_of(mine_ed, other_ed, 0, 2 * RMAX, 0)
    each_peer(lambda p: reducing(p, lambda: rs(0, p, rank).start()))
    for_blocks(lambda b: to_twin(0, b).wait_recv())
    gram_of(mine_ed, other_ed, 0, 2 * RMAX, 1)
    each_peer(lambda p: reducing(p, lambda: rs(1, p, rank).start()))
    place = iota((8, chans), 0)
    for k in range(2):
        aux[...] = jnp.where(place == k, acc[k, chans:chans + 8, :], aux[...])
    each_peer(lambda p: au(p, rank).start())
    aux_all[rank] = aux[...]

    def finish(b):
        pl.when(has_hi)(lambda: dec_up(b).wait_send())
        pl.when(has_lo)(lambda: dec_dn(b).wait_send())
        to_twin(0, b).wait_send()
        to_twin(1, b).wait_send()

    def finish_late(b):
        for_edges(b, lambda c: c.wait_send())

    def finish_early(j):
        pl.when(has_hi)(lambda: far_dec_up(j).wait_send())
        pl.when(has_lo)(lambda: far_dec_dn(j).wait_send())

    for_blocks(finish)
    for_blocks(finish_late, 0, late)
    for_blocks(finish_early, 0, blocks - late)
    sky_up().wait_send()
    sky_dn().wait_send()
    def reduce_own(k):
        shares[k, rank] = acc[k, part_of(rank), :]
        each_peer(lambda p: rs(k, rank, p).wait_recv())
        whole = shares[k, 0]
        whole = lax.fori_loop(1, peers, lambda p, t: t + shares[k, p], whole)
        total[k, part_of(rank), :] = whole
        in_order(lambda p: ag(k, p, rank).start())

    for k in range(2):
        reducing(rank, functools.partial(reduce_own, k))
    each_peer(lambda p: au(p, p).wait_recv())
    each_peer(lambda p: au(p, rank).wait_send())
    for k in range(2):
        each_peer(lambda p: reducing(p, lambda: rs(k, p, rank).wait_send()))
    sums = lax.fori_loop(1, peers, lambda p, t: t + aux_all[p], aux_all[0])
    count = sums[2:3, 0:1]
    means = sums / count
    mean_ref[...] = means[0:1, :]
    column = jnp.transpose(jnp.broadcast_to(means[0:1, :], (chans, chans)))
    for k in range(2):
        each_peer(lambda p: reducing(p, lambda: ag(k, p, p).wait_recv()))
        block = (total[k] - count * column * means[k:k + 1, :]) / (count - 1.0)
        place = band if k == 0 else 1 - band
        cov_ref[pl.ds(pl.multiple_of(place * chans, chans), chans), :] = jnp.transpose(block)

    for k in range(2):
        reducing(rank, lambda: each_peer(lambda p: ag(k, p, rank).wait_send()))


def store(smoothed_ref, mean_ref, cov_ref, smoothed_hbm, mean_hbm, cov_hbm, sems):
    pairs = ((smoothed_ref, smoothed_hbm), (mean_ref, mean_hbm), (cov_ref, cov_hbm))
    copies = [pltpu.make_async_copy(src, dst, sems.at[i]) for i, (src, dst) in enumerate(pairs)]
    for copy in copies:
        copy.start()
    for copy in copies:
        copy.wait()


def per_device(n_ra, n_dec, sky_maps, radii, valid):
    chans, rows, cols = sky_maps.shape
    blocks = chans // CB
    rows8 = up(rows, 16)
    groups = cols // WIDE
    per = -(-rows // groups)
    peers = n_ra * n_dec
    share = chans // min(peers, chans // 8)
    early = early_blocks(blocks)
    far_per = -(-2 * RMAX // groups)
    tall = max(per * groups, rows8)
    f32, b16, dma = jnp.float32, jnp.bfloat16, pltpu.SemaphoreType.DMA
    vmem = pl.BlockSpec(memory_space=pltpu.VMEM)
    hbm = pl.BlockSpec(memory_space=pltpu.HBM)
    in_at, in_rows, edge_rows = inner_rows(rows)
    inner, outer = rows - 2 * RMAX, 2 * RMAX
    flat = pltpu.with_memory_space_constraint(jnp.transpose(sky_maps, (1, 0, 2)), pltpu.HBM)
    radii = pltpu.with_memory_space_constraint(radii, pltpu.HBM)
    valid = pltpu.with_memory_space_constraint(valid, pltpu.HBM)
    packed = pltpu.VMEM((blocks, per, CB, cols), b16)
    far = pltpu.VMEM((early, far_per, CB, cols), b16)
    raw = pltpu.VMEM((RMAX, early * CB, cols), b16)
    edge = pltpu.VMEM((blocks - early, RMAX, CB, cols), b16)
    smoothed, mean, cov = pl.pallas_call(
        functools.partial(kernel, (n_ra, n_dec, rows, chans, cols)),
        out_shape=(
            pltpu.VMEM((rows, chans, cols), b16),
            pltpu.VMEM((1, chans), f32),
            pltpu.VMEM((2 * chans, chans), f32),
        ),
        in_specs=[hbm, hbm, hbm],
        out_specs=(vmem, vmem, vmem),
        scratch_shapes=[
            pltpu.VMEM((rows, chans, cols), b16),
            pltpu.VMEM((rows, cols), jnp.int32),
            pltpu.SMEM((chans,), jnp.int32),
            dma((blocks + 2,)),
            pltpu.VMEM((RMAX + 1, 2 * cols, cols), b16),
            pltpu.VMEM((RMAX + 1, in_rows, 128), b16),
            pltpu.VMEM((RMAX + 1, 2 * edge_rows, 128), b16),
            pltpu.VMEM((tall * CB, cols), f32),
            pltpu.VMEM((tall * CB, cols), f32),
            pltpu.VMEM((rows8 * CB, cols), f32),
            pltpu.VMEM((blocks, 128 * CB, cols), f32),
            pltpu.VMEM((rows, CB, cols), b16),
            pltpu.VMEM((blocks, inner, CB, cols), b16),
            pltpu.VMEM((blocks, outer, CB, cols), b16),
            pltpu.VMEM((blocks, inner, CB, cols), b16),
            pltpu.VMEM((blocks, outer, CB, cols), b16),
            packed, packed, packed, packed,
            far, far, far, far,
            edge, edge, edge, edge, raw, raw,
            pltpu.VMEM((2, chans + CB, chans), f32),
            pltpu.VMEM((2, peers, share, chans), f32),
            pltpu.VMEM((2, chans, chans), f32),
            pltpu.VMEM((8, chans), f32),
            pltpu.VMEM((peers, 8, chans), f32),
            dma((2, blocks + early)), dma((2, blocks + early)),
            dma((2, blocks)), dma((2, blocks)), dma((2, blocks)), dma((2, blocks)),
            dma((2, peers)), dma((2, peers)), dma((2, peers)), dma((2, peers)), dma((peers,)), dma((peers,)),
        ],
        compiler_params=pltpu.CompilerParams(
            collective_id=0, has_side_effects=True, vmem_limit_bytes=40 * 1024 * 1024
        ),
    )(radii, flat, valid)
    smoothed, mean, cov = pl.pallas_call(
        store,
        out_shape=(
            jax.ShapeDtypeStruct((rows, chans, cols), b16),
            jax.ShapeDtypeStruct((1, chans), f32),
            jax.ShapeDtypeStruct((2 * chans, chans), f32),
        ),
        in_specs=(vmem, vmem, vmem),
        out_specs=(hbm, hbm, hbm),
        scratch_shapes=[dma((3,))],
    )(*(pltpu.with_memory_space_constraint(part, pltpu.VMEM) for part in (smoothed, mean, cov)))
    return (jnp.transpose(smoothed, (1, 0, 2)), mean.reshape(chans), cov)


def solution(mesh):
    return jax.shard_map(
        functools.partial(per_device, mesh.shape["ra"], mesh.shape["dec"]),
        mesh=mesh,
        in_specs=(
            P(("groups", "band"), "ra", "dec"),
            P(("groups", "band")),
            P(("groups", "ra"), "dec"),
        ),
        out_specs=(P(("groups", "band"), "ra", "dec"), P(("groups", "band")), P("groups", "band")),
        check_vma=False,
    )
```
